32 devices in a mesh: req: 4 (over y, x), mlp: 8 (over z, core).
Axes of the slice: x: 2, y: 2, z: 4, core: 2. Of those that a mesh axis runs over, the one named last changes fastest.
Arguments:
- prompt_tokens: bfloat16 [8, 1024, 2048], P('req', None, 'mlp'), may hold values from -6 to 6
- decode_tokens: bfloat16 [16, 2048], P('req', 'mlp'), may hold values from -6 to 6
- prompt_lengths: int32 [8], P('req'), may hold values from 128 to 1024, as said below
- decode_states: float32 [16, 16, 128, 128], P('req', 'mlp'), may hold values from -6 to 6
- w_fio: float32 [2048, 6144], P('req', 'mlp'), may hold values from -0.125 to 0.125
- forget_bias: float32 [2048], P('mlp'), as said below
- head_gain: float32 [2048], P('mlp'), may hold values from 0.1 to 1.9
- w_out: float32 [2048, 2048], P('mlp', 'req'), may hold values from -0.125 to 0.125
- mlp_gain: float32 [2048], replicated, may hold values from 0.1 to 1.9
- w_gu: float32 [2048, 11264], P('req', 'mlp'), may hold values from -0.125 to 0.125
- w_down: float32 [5632, 2048], P('mlp', 'req'), may hold values from -0.078125 to 0.078125
Outputs:
- prompt_out: bfloat16 [8, 1024, 2048], P('req', None, 'mlp')
- decode_out: bfloat16 [16, 2048], P('req', 'mlp')
- prompt_states: float32 [8, 16, 128, 128], P('req', 'mlp')
- decode_next: float32 [16, 16, 128, 128], P('req', 'mlp')
The draws below stay inside these ranges and needn't reach their ends.
Inputs may be any that keep to these rules, and one draw needn't show every extreme that they name: `prompt_lengths`: slots at or past a prompt's length are padding; one prompt has length 1024 and another 1024 // 8. `forget_bias`: every entry is at least 3 and at most ln(1024) + 1.7.
All inputs are finite; a program needn't handle non-finite values.
Results may differ from the reference program's by a relative error of at most 0.02.
Values may be sent and summed in bfloat16 or wider, within the bound.
A program may use at most 128 MiB of HBM per device.

```python
import jax
import jax.numpy as jnp
from jax import lax

D = 2048
H = 16
DK = 128
FF = 5632
PLEN = 1024
PROMPTS = 8
DECODES = 16
FF_DEV = 704
N_MLP = 8


def draw_prompt_lengths(key, part):
    first_key = jax.random.fold_in(key, 11)
    second_key = jax.random.fold_in(key, 12)
    drawn = jax.random.randint(first_key, (PROMPTS,), PLEN // 8, PLEN + 1)
    chosen = jax.random.randint(second_key, (), 0, PROMPTS)
    indices = jnp.arange(PROMPTS, dtype=jnp.int32)
    drawn = jnp.where(indices == chosen, PLEN, drawn)
    drawn = jnp.where(indices == (chosen + 1) % PROMPTS, PLEN // 8, drawn)
    return drawn.astype(jnp.int32)


def draw_forget_bias(key, part):
    first_key = jax.random.fold_in(key, 21)
    second_key = jax.random.fold_in(key, 22)
    slow_heads = jax.random.randint(first_key, (H, 1), 0, 2)
    spread = jax.random.uniform(second_key, (H, DK), jnp.float32, 0.0, 1.0)
    slow_value = jnp.log(jnp.float32(PLEN)) + 0.7 + spread
    fast_value = 3.0 + spread
    return jnp.where(slow_heads == 1, slow_value, fast_value).reshape(H * DK).astype(jnp.float32)


def block_scale(rng, shape, cuts, low, high):
    factor_of = 1.0
    for dim, parts in cuts:
        draws = jax.random.uniform(jax.random.fold_in(jax.random.fold_in(rng, 6), dim), (parts,), jnp.float32, low / len(cuts), high / len(cuts))
        factor_of = factor_of * jnp.repeat(jnp.exp(draws), shape[dim] // parts).reshape((-1,) + (1,) * (len(shape) - 1 - dim))
    return factor_of


def gaussian(own_key, extent, width, reach, shards=(), kind=jnp.bfloat16):
    factor_of = block_scale(own_key, extent, shards, -0.22, 0.18) if shards else 1.0
    result = jax.random.normal(own_key, extent, jnp.float32) * width * factor_of
    return jnp.minimum(jnp.maximum(result, -reach), reach).astype(kind)


def setup_inputs(seed: int = 0) -> dict:
    arg_keys = jax.random.split(jax.random.key(seed), 12)
    prompt_tokens = gaussian(arg_keys[0], (PROMPTS, PLEN, D), 1.0, 6.0, ((0, 4), (2, 8)))
    decode_tokens = gaussian(arg_keys[1], (DECODES, D), 1.0, 6.0, ((0, 4), (1, 8)))
    prompt_lengths = draw_prompt_lengths(jax.random.fold_in(arg_keys[11], 71), 0)
    decode_states = gaussian(arg_keys[3], (DECODES, H, DK, DK), 1.0, 6.0, ((0, 4), (1, 8)), jnp.float32)
    w_fio = gaussian(arg_keys[4], (D, 3 * H * DK), D ** -0.5, 0.125, ((0, 4), (1, 8)), jnp.float32)
    forget_bias = draw_forget_bias(jax.random.fold_in(arg_keys[11], 71), 0)
    head_gain = jnp.clip(1.0 + 0.18 * jax.random.normal(arg_keys[6], (H * DK,), jnp.float32), 0.1, 1.9)
    w_out = gaussian(arg_keys[7], (H * DK, D), (H * DK) ** -0.5, 0.125, ((0, 8), (1, 4)), jnp.float32)
    mlp_gain = jnp.clip(1.0 + 0.18 * jax.random.normal(arg_keys[8], (D,), jnp.float32), 0.1, 1.9)
    w_gu = gaussian(arg_keys[9], (D, 2 * FF), D ** -0.5, 0.125, ((0, 4), (1, 8)), jnp.float32)
    w_down = gaussian(arg_keys[10], (FF, D), FF ** -0.5, 0.078125, ((0, 8), (1, 4)), jnp.float32)
    return {"prompt_tokens": prompt_tokens, "decode_tokens": decode_tokens, "prompt_lengths": prompt_lengths, "decode_states": decode_states, "w_fio": w_fio, "forget_bias": forget_bias, "head_gain": head_gain, "w_out": w_out, "mlp_gain": mlp_gain, "w_gu": w_gu, "w_down": w_down}


epsilon = 1e-05

def head_norm(source_rows, scales):
    mean_square = lax.optimization_barrier(jnp.mean(source_rows * source_rows, axis=-1, keepdims=True))
    return source_rows * lax.rsqrt(mean_square + epsilon) * scales

def reference(prompt_tokens, decode_tokens, prompt_lengths, decode_states, w_fio, forget_bias, head_gain, w_out, mlp_gain, w_gu, w_down):
    prompt_rows = PROMPTS * PLEN
    x_rows = jnp.concatenate([prompt_tokens.reshape(prompt_rows, D), decode_tokens], axis=0)
    mixing = jnp.dot(x_rows, w_fio.astype(jnp.bfloat16), preferred_element_type=jnp.float32)
    mixing = mixing.reshape(-1, H, 3, DK)
    bias_table = forget_bias.reshape(H, DK)
    forget_logit = mixing[:, :, 0] + bias_table
    values = mixing[:, :, 1]
    queries = mixing[:, :, 2]

    def time_first(source_array):
        return source_array[:prompt_rows].reshape(PROMPTS, PLEN, H, DK).transpose(1, 0, 2, 3)
    alive_mask = jnp.arange(PLEN, dtype=jnp.int32)[:, None] < prompt_lengths[None, :]

    def advance(carried, inputs):
        forget_now, value_now, query_now, alive_now = inputs
        alive_wide = alive_now[:, None, None]
        forget_gate = jnp.where(alive_wide, jax.nn.sigmoid(forget_now), 1.0)
        key_gate = jnp.where(alive_wide, jax.nn.sigmoid(-forget_now), 0.0)
        carried = forget_gate[..., None] * carried + key_gate[..., None] * value_now[:, :, None, :]
        emitted = jnp.einsum('phcv,phc->phv', carried, query_now, precision=lax.Precision.HIGHEST)
        emitted = jnp.where(alive_wide, emitted, 0.0)
        return (carried, emitted)
    start_state = jnp.zeros((PROMPTS, H, DK, DK), jnp.float32)
    prompt_states, prompt_mixed = lax.scan(advance, start_state, (time_first(forget_logit), time_first(values), time_first(queries), alive_mask))
    prompt_mixed = prompt_mixed.transpose(1, 0, 2, 3).reshape(prompt_rows, H, DK)
    decode_logit = forget_logit[prompt_rows:]
    decode_next = jax.nn.sigmoid(decode_logit)[..., None] * decode_states + jax.nn.sigmoid(-decode_logit)[..., None] * values[prompt_rows:][:, :, None, :]
    decode_mixed = jnp.einsum('nhcv,nhc->nhv', decode_next, queries[prompt_rows:], precision=lax.Precision.HIGHEST)
    mixed_all = jnp.concatenate([prompt_mixed, decode_mixed], axis=0)
    head_rows = head_norm(mixed_all, head_gain.reshape(H, DK)).astype(jnp.bfloat16).reshape(-1, H * DK)
    attention = jnp.dot(head_rows, w_out.astype(jnp.bfloat16), preferred_element_type=jnp.float32)
    residual = (x_rows.astype(jnp.float32) + attention).astype(jnp.bfloat16)
    residual_wide = residual.astype(jnp.float32)
    normed = (head_norm(residual_wide, 1.0) * mlp_gain).astype(jnp.bfloat16)
    gate_up = jnp.dot(normed, w_gu.astype(jnp.bfloat16), preferred_element_type=jnp.float32)
    gate_up = gate_up.reshape(-1, N_MLP, 2, FF_DEV)
    gate_part = gate_up[:, :, 0].reshape(-1, FF)
    up_part = gate_up[:, :, 1].reshape(-1, FF)
    hidden = (jax.nn.silu(gate_part) * up_part).astype(jnp.bfloat16)
    total_rows = hidden.shape[0]
    hidden_blocks = hidden.reshape(total_rows, N_MLP, FF_DEV).transpose(1, 0, 2)
    down_blocks = w_down.astype(jnp.bfloat16).reshape(N_MLP, FF_DEV, D)

    def add_block(running, pair):
        hidden_block, down_block = pair
        part_sum = jnp.dot(hidden_block, down_block, preferred_element_type=jnp.float32).astype(jnp.bfloat16)
        part_sum = lax.optimization_barrier(part_sum)
        return (running + part_sum.astype(jnp.float32), None)
    down_total, unused = lax.scan(add_block, jnp.zeros((total_rows, D), jnp.float32), (hidden_blocks, down_blocks))
    layer_output = (residual_wide + down_total).astype(jnp.bfloat16)
    return (layer_output[:prompt_rows].reshape(PROMPTS, PLEN, D), layer_output[prompt_rows:], prompt_states, decode_next)
```

```python
import functools

import jax
import jax.numpy as jnp
import numpy as np
from jax import lax
from jax.experimental import pallas as pl
from jax.experimental.pallas import tpu as pltpu
from jax.sharding import PartitionSpec as P

MESH = pl.DeviceIdType.MESH
EPS = 1e-05
SUB = 128
LEVELS = 7
CHUNK = 256
DEC = 16
BF = jnp.bfloat16
F32 = jnp.float32


def decay_sums():
    t = np.arange(SUB)[:, None]
    s = np.arange(SUB)[None, :]
    parts = [s <= t, s > t]
    for level in range(1, LEVELS + 1):
        block = 1 << level
        middle = (t // block) * block + block // 2 - 1
        parts.append(((s > middle) & (s <= t)) | ((s > t) & (s <= middle)))
    stacked = np.concatenate(parts, axis=0).astype(np.float32)
    return np.concatenate([stacked, stacked], axis=1)


def dot(a, b, dims=((1,), (0,))):
    return lax.dot_general(a, b, (dims, ((), ())), preferred_element_type=F32)


class Exchange:
    def __init__(self, x_ref, d_ref, full, dfull, sib_out, sib_in, z_out, z_in, keep,
                 dsib_out, dsib_in, dz_out, dz_in, dkeep, sems, extra_peers=False):
        self.req = lax.axis_index("req")
        self.me = lax.axis_index("mlp")
        self.n_req = lax.axis_size("req")
        self.chips = lax.axis_size("mlp") // 2
        self.chip = self.me // 2
        self.core = self.me % 2
        self.x, self.d = x_ref, d_ref
        self.full, self.dfull = full, dfull
        self.bufs = (sib_out, sib_in, z_out, z_in, keep)
        self.dbufs = (dsib_out, dsib_in, dz_out, dz_in, dkeep)
        (self.ga_s, self.ga_r, self.gr_s, self.sb_s, self.sb_r, self.z_s, self.z_r) = sems
        self.extra = extra_peers
        self.count = x_ref.shape[0] // CHUNK

    def sibling(self):
        return (self.req, self.chip * 2 + 1 - self.core)

    def far(self, o):
        j = lax.rem(self.chip + o, self.chips)
        return j, (self.req, j * 2 + self.core)

    def enter(self):
        barrier = pltpu.get_barrier_semaphore()
        peers = [self.sibling()] + [self.far(o)[1] for o in range(1, self.chips)]
        if self.extra:
            peers += [(lax.rem(self.req + o, self.n_req), self.me) for o in range(1, self.n_req)]
        for peer in peers:
            pl.semaphore_signal(barrier, inc=1, device_id=peer, device_id_type=MESH)
        pl.semaphore_wait(barrier, len(peers))

    def rows(self, k):
        return pl.ds(pl.multiple_of(k * CHUNK, CHUNK), CHUNK)

    def own(self, k, dec):
        return self.d if dec else self.x.at[self.rows(k)]

    def slot(self, k, src, dec):
        return self.dfull.at[src] if dec else self.full.at[src, self.rows(k)]

    def remote(self, src, dst, ssem, rsem, dev):
        return pltpu.make_async_remote_copy(
            src_ref=src, dst_ref=dst, send_sem=ssem, recv_sem=rsem, device_id=dev, device_id_type=MESH)

    def gather_copy(self, k, o, dec):
        dev = self.sibling() if o == 0 else self.far(o)[1]
        return self.remote(self.own(k, dec), self.slot(k, self.me, dec),
                           self.ga_s.at[k, o], self.ga_r.at[k, self.me], dev)

    def relay_copy(self, k, o, dec):
        src = self.far(o)[0] * 2 + self.core
        return self.remote(self.slot(k, src, dec), self.slot(k, src, dec),
                           self.gr_s.at[k, o], self.ga_r.at[k, src], self.sibling())

    def arrive(self, k, src, dec):
        slot = self.slot(k, src, dec)
        self.remote(slot, slot, self.gr_s.at[k, 0], self.ga_r.at[k, src], self.sibling()).wait_recv()

    def gather_start(self, k, dec=False):
        for o in range(1, self.chips):
            self.gather_copy(k, o, dec).start()
        self.gather_copy(k, 0, dec).start()
        if dec:
            self.dfull[self.me] = self.d[...]
        else:
            self.full[self.me, self.rows(k), :] = self.x[self.rows(k), :]

    def relay(self, k, dec=False):
        for o in range(1, self.chips):
            self.arrive(k, self.far(o)[0] * 2 + self.core, dec)
            self.relay_copy(k, o, dec).start()

    def gather_done(self, k, dec=False):
        for j in range(self.chips):
            self.arrive(k, j * 2 + 1 - self.core, dec)

    def sib_copy(self, k, dec):
        b = self.dbufs if dec else self.bufs
        src, dst = (b[0], b[1]) if dec else (b[0].at[k], b[1].at[k])
        return self.remote(src, dst, self.sb_s.at[k], self.sb_r.at[k], self.sibling())

    def share(self, k, operand, weights, dec=False):
        b = self.dbufs if dec else self.bufs
        par = lax.rem(k, 2)
        for j in range(self.chips):
            term = dot(operand, weights[j * 2 + 1 - self.core]).astype(BF)
            if dec:
                b[0][j] = term
            else:
                b[0][k, j] = term
        self.sib_copy(k, dec).start()
        for j in range(self.chips):
            term = dot(operand, weights[j * 2 + self.core])
            if dec:
                b[4][j] = term
            else:
                b[4][par, j] = term

    def z_copy(self, k, o, dec):
        b = self.dbufs if dec else self.bufs
        j, dev = self.far(o)
        src = b[2].at[j] if dec else b[2].at[k, j]
        dst = b[3].at[self.chip] if dec else b[3].at[k, self.chip]
        return self.remote(src, dst, self.z_s.at[k, o], self.z_r.at[k, self.chip], dev)

    def z_wait(self, k, o, dec):
        b = self.dbufs if dec else self.bufs
        j, dev = self.far(o)
        ref = b[3].at[j] if dec else b[3].at[k, j]
        self.remote(ref, ref, self.z_s.at[k, o], self.z_r.at[k, j], dev).wait_recv()

    def pair_sum(self, k, dec=False):
        b = self.dbufs if dec else self.bufs
        par = lax.rem(k, 2)
        self.sib_copy(k, dec).wait_recv()
        for o in list(range(1, self.chips)) + [0]:
            j = lax.rem(self.chip + o, self.chips)
            if dec:
                b[2][j] = (b[4][j] + b[1][j].astype(F32)).astype(BF)
            else:
                b[2][k, j] = (b[4][par, j] + b[1][k, j].astype(F32)).astype(BF)
            if o:
                self.z_copy(k, o, dec).start()

    def total(self, k, dec=False):
        b = self.dbufs if dec else self.bufs
        x = (self.d[...] if dec else self.x[self.rows(k), :]).astype(F32)
        acc = (b[2][self.chip] if dec else b[2][k, self.chip]).astype(F32)
        for o in range(1, self.chips):
            self.z_wait(k, o, dec)
            j = self.far(o)[0]
            acc = acc + (b[3][j] if dec else b[3][k, j]).astype(F32)
        return (x + acc).astype(BF)

    def finish(self, k, dec=False):
        for o in range(self.chips):
            self.gather_copy(k, o, dec).wait_send()
        for o in range(1, self.chips):
            self.relay_copy(k, o, dec).wait_send()
            self.z_copy(k, o, dec).wait_send()
        self.sib_copy(k, dec).wait_send()

    def run(self, work, out_ref, dout_ref, before=None):
        count = self.count
        self.enter()
        if before is not None:
            before()
        lax.fori_loop(0, count, lambda k, c: (self.gather_start(k), c)[1], 0)
        self.gather_start(count, True)
        self.relay(0)

        def body(k, c):
            @pl.when(k + 1 < count)
            def _():
                self.relay(k + 1)
            self.gather_done(k)
            work(k, False)

            @pl.when(k > 0)
            def _():
                self.pair_sum(k - 1)
            return c

        lax.fori_loop(0, count, body, 0)
        self.relay(count, True)
        self.gather_done(count, True)
        self.pair_sum(count - 1)
        work(count, True)
        self.pair_sum(count, True)

        def last(k, c):
            out_ref[self.rows(k), :] = self.total(k)
            self.finish(k)
            return c

        lax.fori_loop(0, count, last, 0)
        dout_ref[...] = self.total(count, True)
        self.finish(count, True)


def gates(z):
    u = jnp.exp(-jnp.abs(z))
    big = 1.0 / (1.0 + u)
    small = u * big
    logf = jnp.minimum(z, 0.0) - jnp.log1p(u)
    return logf, jnp.where(z >= 0, small, big), jnp.where(z >= 0, big, small)


def head_norm(o, gain):
    return (o * lax.rsqrt(jnp.mean(o * o, axis=-1, keepdims=True) + EPS) * gain).astype(BF)


def mix_kernel(heads, plen, lengths, x_ref, d_ref, wf_ref, wo_ref, bias_ref, gain_ref, sums_ref, dst_ref,
               out_ref, dout_ref, states_ref, next_ref,
               wf, wo, state, ws_s, ws_r, full, dfull, *rest):
    ex = Exchange(x_ref, d_ref, full, dfull, *rest[:10], rest[10:], extra_peers=True)
    n_mlp, feat = full.shape[0], full.shape[2]
    per = wf_ref.shape[0] // feat
    dk = dst_ref.shape[-1]
    decodes = dst_ref.shape[0]
    req = ex.req

    def w_copy(i, o, mine):
        peer = lax.rem(req + o, ex.n_req)
        owner = req if mine else peer
        ref = wo.at[pl.ds(owner * per, per)] if i else wf.at[owner]
        return ex.remote(ref, ref, ws_s.at[i, o], ws_r.at[i, owner], (peer, ex.me))

    def before():
        wf[req] = wf_ref[...].astype(BF)
        for p in range(per):
            wo[req * per + p] = wo_ref[:, p * feat:(p + 1) * feat].astype(BF)
        for i in range(2):
            for o in range(1, ex.n_req):
                w_copy(i, o, True).start()

    def mixing(block):
        acc = None
        for s in range(n_mlp):
            term = dot(block(s), wf[s // per, (s % per) * feat:(s % per + 1) * feat, :])
            acc = term if acc is None else acc + term
        return acc

    def step(m, k, sub):
        p = (k * CHUNK) // plen
        row0 = lax.rem(k * CHUNK, plen) + sub * SUB
        row = row0 + lax.broadcasted_iota(jnp.int32, (SUB, dk), 0)
        alive = row < lengths[p]
        lg, kg = [], []
        for h in range(heads):
            z = m[:, h * 3 * dk:h * 3 * dk + dk] + bias_ref[:, h * dk:(h + 1) * dk]
            logf, key, _ = gates(z)
            lg.append(jnp.where(alive, logf, 0.0))
            kg.append(jnp.where(alive, key, 0.0))
        lf = jnp.concatenate(lg, axis=1) if heads > 1 else lg[0]
        hi = lf.astype(BF)
        lo = (lf - hi.astype(F32)).astype(BF)
        decays = jnp.exp(dot(sums_ref[...], jnp.concatenate([hi, lo], axis=0)))
        t = lax.broadcasted_iota(jnp.int32, (SUB, SUB), 0)
        s = lax.broadcasted_iota(jnp.int32, (SUB, SUB), 1)
        outs = []
        for h in range(heads):
            cols = slice(h * dk, (h + 1) * dk)
            v = m[:, h * 3 * dk + dk:h * 3 * dk + 2 * dk]
            q = m[:, h * 3 * dk + 2 * dk:h * 3 * dk + 3 * dk]
            k_ = kg[h]
            v16 = v.astype(BF)
            head = decays[0:SUB, cols]
            tail = decays[SUB:2 * SUB, cols]
            old = jnp.where(row0 == 0, 0.0, state[h])
            o = dot((q * head).astype(BF), old.astype(BF), ((1,), (1,)))
            scores = None
            for level in range(LEVELS, 0, -1):
                e = decays[(level + 1) * SUB:(level + 2) * SUB, cols]
                right = (lax.broadcasted_iota(jnp.int32, (SUB, dk), 0) >> (level - 1)) & 1
                qt = jnp.where(right == 1, q * e, 0.0).astype(BF)
                kt = jnp.where(right == 1, 0.0, k_ * e).astype(BF)
                term = dot(qt, kt, ((1,), (1,)))
                if level == LEVELS:
                    scores = term
                else:
                    scores = scores + jnp.where((t >> level) == (s >> level), term, 0.0)
            o = o + dot(scores.astype(BF), v16)
            o = o + jnp.sum(q * k_, axis=-1, keepdims=True) * v
            outs.append(jnp.where(alive, o, 0.0))
            new = old * head[SUB - 1:SUB, :] + dot(v16, (k_ * tail).astype(BF), ((0,), (0,)))
            state[h] = new
            states_ref[p, h] = new.T
        return outs

    def normed(outs):
        rows = [head_norm(o, gain_ref[:, h * dk:(h + 1) * dk]) for h, o in enumerate(outs)]
        return jnp.concatenate(rows, axis=1) if heads > 1 else rows[0]

    def decode(m):
        outs = []
        pad = jnp.zeros((dk - DEC, dk), F32)
        for h in range(heads):
            z = m[:, h * 3 * dk:h * 3 * dk + dk] + bias_ref[:, h * dk:(h + 1) * dk]
            _, key, f = gates(z)
            v = m[:, h * 3 * dk + dk:h * 3 * dk + 2 * dk]
            q = m[:, h * 3 * dk + 2 * dk:h * 3 * dk + 3 * dk]
            f_t = jnp.concatenate([f, pad], axis=0).T
            k_t = jnp.concatenate([key, pad], axis=0).T
            q_t = jnp.concatenate([q, pad], axis=0).T
            rows = []
            for n in range(decodes):
                new = f_t[:, n:n + 1] * dst_ref[n, h] + k_t[:, n:n + 1] * v[n:n + 1, :]
                next_ref[n, h] = new
                rows.append(jnp.sum(q_t[:, n:n + 1] * new, axis=0, keepdims=True))
            rows.append(jnp.zeros((DEC - decodes, dk), F32))
            outs.append(jnp.concatenate(rows, axis=0))
        return normed(outs)

    def work(k, dec):
        if dec:
            m = mixing(lambda s: dfull[s])
            ex.share(k, decode(m), wo, True)
            return

        @pl.when(k == 0)
        def _():
            for o in range(1, ex.n_req):
                for i in range(2):
                    w_copy(i, o, False).wait_recv()
        m = mixing(lambda s: full[s, ex.rows(k), :])
        pieces = [normed(step(m[i * SUB:(i + 1) * SUB], k, i)) for i in range(CHUNK // SUB)]
        ex.share(k, jnp.concatenate(pieces, axis=0), wo)

    ex.run(work, out_ref, dout_ref, before)
    for o in range(1, ex.n_req):
        for i in range(2):
            w_copy(i, o, True).wait_send()


def mlp_kernel(x_ref, d_ref, gain_ref, wgu, wd, out_ref, dout_ref, full, dfull, *rest):
    ex = Exchange(x_ref, d_ref, full, dfull, *rest[:10], rest[10:])
    n_mlp, feat = full.shape[0], full.shape[2]
    per = wgu.shape[2] // feat
    width = n_mlp * feat

    def work(k, dec):
        def block(s):
            return (dfull[s] if dec else full[s, ex.rows(k), :]).astype(F32)
        total = None
        for s in range(n_mlp):
            x = block(s)
            part = jnp.sum(x * x, axis=-1, keepdims=True)
            total = part if total is None else total + part
        scale = lax.rsqrt(total / width + EPS)
        gate = up = None
        for s in range(n_mlp):
            x = (block(s) * scale * gain_ref[:, s * feat:(s + 1) * feat]).astype(BF)
            part = slice((s % per) * feat, (s % per + 1) * feat)
            g = dot(x, wgu[s // per, 0, part, :])
            u = dot(x, wgu[s // per, 1, part, :])
            gate = g if gate is None else gate + g
            up = u if up is None else up + u
        hidden = (gate / (1.0 + jnp.exp(-gate)) * up).astype(BF)
        ex.share(k, hidden, wd, dec)

    ex.run(work, out_ref, dout_ref)


def exchange_scratch(n_mlp, count, feat):
    chips = n_mlp // 2
    dma = pltpu.SemaphoreType.DMA
    big = pltpu.VMEM((count, chips, CHUNK, feat), BF)
    small = pltpu.VMEM((chips, DEC, feat), BF)
    return [
        pltpu.VMEM((n_mlp, count * CHUNK, feat), BF),
        pltpu.VMEM((n_mlp, DEC, feat), BF),
        big, big, big, big, pltpu.VMEM((2, chips, CHUNK, feat), F32),
        small, small, small, small, pltpu.VMEM((chips, DEC, feat), F32),
        dma((count + 1, chips)), dma((count + 1, n_mlp)), dma((count + 1, chips)),
        dma((count + 1,)), dma((count + 1,)), dma((count + 1, chips)), dma((count + 1, chips)),
    ]


def on_device(n_req, n_mlp, prompt_tokens, decode_tokens, prompt_lengths, decode_states, w_fio, forget_bias,
              head_gain, w_out, mlp_gain, w_gu, w_down):
    prompts, plen, feat = prompt_tokens.shape
    decodes, heads, dk, _ = decode_states.shape
    rows = prompts * plen
    count = rows // CHUNK
    per = w_fio.shape[0] // feat
    vmem = pl.BlockSpec(memory_space=pltpu.VMEM)
    x = prompt_tokens.reshape(rows, feat)
    d = jnp.pad(decode_tokens, ((0, DEC - decodes), (0, 0)))
    params = functools.partial(pltpu.CompilerParams, has_side_effects=True, vmem_limit_bytes=58 * 2**20)
    hidden = w_down.shape[0]

    gu = w_gu.astype(BF).reshape(w_gu.shape[0], 2, hidden).transpose(1, 0, 2)
    gu = lax.all_gather(gu, "req", axis=0)
    down = w_down.astype(BF).reshape(hidden, per, feat).transpose(1, 0, 2)
    down = lax.all_gather(down, "req", axis=0, tiled=True)

    dma = pltpu.SemaphoreType.DMA
    residual, dresidual, states, after = pl.pallas_call(
        functools.partial(mix_kernel, heads, plen),
        out_shape=(
            jax.ShapeDtypeStruct((rows, feat), BF),
            jax.ShapeDtypeStruct((DEC, feat), BF),
            jax.ShapeDtypeStruct((prompts, heads, dk, dk), F32),
            jax.ShapeDtypeStruct((decodes, heads, dk, dk), F32),
        ),
        in_specs=[pl.BlockSpec(memory_space=pltpu.SMEM)] + [vmem] * 8,
        out_specs=(vmem,) * 4,
        scratch_shapes=[
            pltpu.VMEM((n_req,) + w_fio.shape, BF),
            pltpu.VMEM((n_mlp, heads * dk, feat), BF),
            pltpu.VMEM((heads, dk, dk), F32),
            dma((2, n_req)), dma((2, n_req)),
        ] + exchange_scratch(n_mlp, count, feat),
        compiler_params=params(collective_id=0),
        name="mix",
    )(prompt_lengths, x, d, w_fio, w_out, forget_bias.reshape(1, -1), head_gain.reshape(1, -1),
      jnp.asarray(decay_sums(), BF), decode_states)

    out, dout = pl.pallas_call(
        mlp_kernel,
        out_shape=(jax.ShapeDtypeStruct((rows, feat), BF), jax.ShapeDtypeStruct((DEC, feat), BF)),
        in_specs=[vmem] * 5,
        out_specs=(vmem,) * 2,
        scratch_shapes=exchange_scratch(n_mlp, count, feat),
        compiler_params=params(collective_id=1),
        name="mlp",
    )(residual, dresidual, mlp_gain.reshape(1, -1), gu, down)
    return out.reshape(prompts, plen, feat), dout[:decodes], states, after


def solution(mesh):
    placed = (
        P("req", None, "mlp"),
        P("req", "mlp"),
        P("req"),
        P("req", "mlp", None, None),
        P("req", "mlp"),
        P("mlp"),
        P("mlp"),
        P("mlp", "req"),
        P(),
        P("req", "mlp"),
        P("mlp", "req"),
    )
    return jax.shard_map(
        functools.partial(on_device, mesh.shape["req"], mesh.shape["mlp"]),
        mesh=mesh,
        in_specs=placed,
        out_specs=(
            P("req", None, "mlp"),
            P("req", "mlp"),
            P("req", "mlp", None, None),
            P("req", "mlp", None, None),
        ),
        check_vma=False,
    )
```

```python
import functools

import jax
import jax.numpy as jnp
import numpy as np
from jax import lax
from jax.experimental import pallas as pl
from jax.experimental.pallas import tpu as pltpu
from jax.sharding import PartitionSpec as P

MESH = pl.DeviceIdType.MESH
EPS = 1e-05
SUB = 128
LEVELS = 7
CHUNK = 256
DEC = 16
BF = jnp.bfloat16
F32 = jnp.float32


def decay_sums():
    t = np.arange(SUB)[:, None]
    s = np.arange(SUB)[None, :]
    parts = [s <= t, s > t]
    for level in range(1, LEVELS + 1):
        block = 1 << level
        middle = (t // block) * block + block // 2 - 1
        parts.append(((s > middle) & (s <= t)) | ((s > t) & (s <= middle)))
    stacked = np.concatenate(parts, axis=0).astype(np.float32)
    return np.concatenate([stacked, stacked], axis=1)


def dot(a, b, dims=((1,), (0,))):
    return lax.dot_general(a, b, (dims, ((), ())), preferred_element_type=F32)


class Exchange:
    def __init__(self, x_ref, d_ref, full, dfull, bufs, dbufs, tot, sems, extra_peers=False):
        self.req = lax.axis_index("req")
        self.me = lax.axis_index("mlp")
        self.n_req = lax.axis_size("req")
        self.chips = lax.axis_size("mlp") // 2
        self.chip = self.me // 2
        self.core = self.me % 2
        self.x, self.d = x_ref, d_ref
        self.full, self.dfull = full, dfull
        self.sib_out, self.sib_in, self.sums, self.z_in, self.keep = bufs
        self.dbufs = dbufs
        self.tot = tot
        (self.line_s, self.pair_s, self.got, self.dga_s, self.dgr_s, self.dgot,
         self.sb_s, self.sb_r, self.z_s, self.z_r, self.dz_s, self.dz_r) = sems
        self.extra = extra_peers
        self.count = x_ref.shape[0] // CHUNK

    def sibling(self):
        return (self.req, self.chip * 2 + 1 - self.core)

    def far(self, o):
        j = lax.rem(self.chip + o, self.chips)
        return j, (self.req, j * 2 + self.core)

    def beside(self, right):
        j = self.chip + (1 if right else -1)
        return (self.req, j * 2 + self.core)

    def enter(self):
        barrier = pltpu.get_barrier_semaphore()
        peers = [self.sibling()] + [self.far(o)[1] for o in range(1, self.chips)]
        if self.extra:
            peers += [(lax.rem(self.req + o, self.n_req), self.me) for o in range(1, self.n_req)]
        for peer in peers:
            pl.semaphore_signal(barrier, inc=1, device_id=peer, device_id_type=MESH)
        pl.semaphore_wait(barrier, len(peers))

    def rows(self, k):
        return pl.ds(pl.multiple_of(k * CHUNK, CHUNK), CHUNK)

    def remote(self, src, dst, ssem, rsem, dev):
        return pltpu.make_async_remote_copy(
            src_ref=src, dst_ref=dst, send_sem=ssem, recv_sem=rsem, device_id=dev, device_id_type=MESH)


    def has(self, right):
        return self.chip + 1 < self.chips if right else self.chip > 0

    def block_copy(self, k, h, from_left, to):
        src_chip = self.chip - h if from_left else self.chip + h
        source = src_chip * 2 + self.core
        slot = self.full.at[source, self.rows(k)]
        src = slot if h else self.x.at[self.rows(k)]
        if to == "line":
            sem = self.line_s.at[k, self.chips if h == 0 and not from_left else src_chip]
            dev = self.beside(from_left)
        else:
            sem, dev = self.pair_s.at[k, src_chip], self.sibling()
        return self.remote(src, slot, sem, self.got.at[k, source], dev)

    def each_send(self, k, h, act):
        for from_left in (True, False):
            there = self.chip - h >= 0 if from_left else self.chip + h < self.chips

            def go(from_left=from_left):
                if h and act == "start":
                    source = (self.chip - h if from_left else self.chip + h) * 2 + self.core
                    slot = self.full.at[source, self.rows(k)]
                    self.remote(slot, slot, self.pair_s.at[k, 0], self.got.at[k, source], self.sibling()).wait_recv()

                @pl.when(self.has(from_left))
                def _():
                    copy = self.block_copy(k, h, from_left, "line")
                    copy.start() if act == "start" else copy.wait_send()
                if h or from_left:
                    copy = self.block_copy(k, h, from_left, "pair")
                    copy.start() if act == "start" else copy.wait_send()
            if h:
                pl.when(there)(go)
            else:
                go()

    def hop(self, k, h):
        self.each_send(k, h, "start")
        if h == 0:
            self.full[self.me, self.rows(k), :] = self.x[self.rows(k), :]

    def gather_done(self, k):
        for j in range(self.chips):
            source = j * 2 + 1 - self.core
            slot = self.full.at[source, self.rows(k)]
            self.remote(slot, slot, self.pair_s.at[k, 0], self.got.at[k, source], self.sibling()).wait_recv()


    def dgather_copy(self, o):
        dev = self.sibling() if o == 0 else self.far(o)[1]
        return self.remote(self.d, self.dfull.at[self.me], self.dga_s.at[o], self.dgot.at[self.me], dev)

    def drelay_copy(self, o):
        src = self.far(o)[0] * 2 + self.core
        return self.remote(self.dfull.at[src], self.dfull.at[src], self.dgr_s.at[o], self.dgot.at[src], self.sibling())

    def darrive(self, src):
        slot = self.dfull.at[src]
        self.remote(slot, slot, self.dgr_s.at[0], self.dgot.at[src], self.sibling()).wait_recv()

    def dgather_start(self):
        for o in range(self.chips):
            self.dgather_copy(o).start()
        self.dfull[self.me] = self.d[...]

    def drelay(self):
        for o in range(1, self.chips):
            self.darrive(self.far(o)[0] * 2 + self.core)
            self.drelay_copy(o).start()

    def dgather_done(self):
        for j in range(self.chips):
            self.darrive(j * 2 + 1 - self.core)


    def sib_copy(self, k, dec):
        src, dst = self.dbufs[:2] if dec else (self.sib_out.at[k], self.sib_in.at[k])
        return self.remote(src, dst, self.sb_s.at[k], self.sb_r.at[k], self.sibling())

    def share(self, k, operand, weights, dec=False):
        par = lax.rem(k, 2)
        for j in range(self.chips):
            term = dot(operand, weights[j * 2 + 1 - self.core]).astype(BF)
            if dec:
                self.dbufs[0][j] = term
            else:
                self.sib_out[k, j] = term
        self.sib_copy(k, dec).start()
        for j in range(self.chips):
            term = dot(operand, weights[j * 2 + self.core])
            if dec:
                self.dbufs[4][j] = term
            else:
                self.keep[par, j] = term

    def pair_sum(self, k):
        par = lax.rem(k, 2)
        self.sib_copy(k, False).wait_recv()
        for j in range(self.chips):
            self.sums[k, j] = (self.keep[par, j] + self.sib_in[k, j].astype(F32)).astype(BF)

    def sum_copy(self, k, j, right):
        place = j if right else jnp.where(self.chip - 1 == j, self.chips, j)
        return self.remote(self.sums.at[k, j], self.z_in.at[k, place], self.z_s.at[k, j], self.z_r.at[k, place],
                           self.beside(right))

    def sum_wait(self, k, place):
        ref = self.z_in.at[k, place]
        self.remote(ref, ref, self.z_s.at[k, 0], self.z_r.at[k, place], self.sibling()).wait_recv()

    def chain(self, k, right):
        for j in range(self.chips):
            @pl.when(self.chip < j if right else self.chip > j)
            def _():
                @pl.when(self.has(not right))
                def _():
                    self.sum_wait(k, j)
                    self.sums[k, j] = (self.sums[k, j].astype(F32) + self.z_in[k, j].astype(F32)).astype(BF)
                self.sum_copy(k, j, right).start()

    def total(self, k, out_ref):
        self.tot[...] = self.x[self.rows(k), :].astype(F32) + self.sums[k, self.chip].astype(F32)
        for right, place in ((False, self.chip), (True, self.chips)):
            @pl.when(self.has(right))
            def _():
                self.sum_wait(k, place)
                self.tot[...] += self.z_in[k, place].astype(F32)
        out_ref[self.rows(k), :] = self.tot[...].astype(BF)

    def dz_copy(self, o):
        j, dev = self.far(o)
        return self.remote(self.dbufs[2].at[j], self.dbufs[3].at[self.chip], self.dz_s.at[o],
                           self.dz_r.at[self.chip], dev)

    def dpair_sum(self):
        b = self.dbufs
        self.sib_copy(self.count, True).wait_recv()
        for o in list(range(1, self.chips)) + [0]:
            j = self.far(o)[0]
            b[2][j] = (b[4][j] + b[1][j].astype(F32)).astype(BF)
            if o:
                self.dz_copy(o).start()

    def dtotal(self, out_ref):
        b = self.dbufs
        acc = self.d[...].astype(F32) + b[2][self.chip].astype(F32)
        for o in range(1, self.chips):
            j, dev = self.far(o)
            ref = b[3].at[j]
            self.remote(ref, ref, self.dz_s.at[o], self.dz_r.at[j], dev).wait_recv()
            acc = acc + b[3][j].astype(F32)
        out_ref[...] = acc.astype(BF)
        for o in range(self.chips):
            self.dgather_copy(o).wait_send()
        for o in range(1, self.chips):
            self.drelay_copy(o).wait_send()
            self.dz_copy(o).wait_send()
        self.sib_copy(self.count, True).wait_send()

    def finish(self, k):
        for h in range(self.chips):
            self.each_send(k, h, "wait")
        self.sib_copy(k, False).wait_send()
        for j in range(self.chips):
            for right in (True, False):
                @pl.when(self.chip < j if right else self.chip > j)
                def _():
                    self.sum_copy(k, j, right).wait_send()

    def run(self, work, out_ref, dout_ref, before=None):
        count, chips = self.count, self.chips

        def at(k, action):
            @pl.when((k >= 0) & (k < count))
            def _():
                action(k)

        self.enter()
        if before is not None:
            before()
        self.dgather_start()

        def body(step, c):
            i = step - chips
            for h in range(chips):
                at(i + chips - h, functools.partial(self.hop, h=h))
            pl.when(i == 1)(self.drelay)

            def compute(k):
                self.gather_done(k)
                work(k, False)
            at(i, compute)

            @pl.when(i == 2)
            def _():
                self.dgather_done()
                work(count, True)
            pl.when(i == 3)(self.dpair_sum)
            at(i - 1, self.pair_sum)
            at(i - 1 - self.chip, functools.partial(self.chain, right=True))
            at(i - chips + self.chip, functools.partial(self.chain, right=False))
            at(i - chips - 1, functools.partial(self.total, out_ref=out_ref))
            return c

        lax.fori_loop(0, count + 2 * chips + 1, body, 0)
        self.dtotal(dout_ref)
        lax.fori_loop(0, count, lambda k, c: (self.finish(k), c)[1], 0)


def gates(z):
    u = jnp.exp(-jnp.abs(z))
    big = 1.0 / (1.0 + u)
    small = u * big
    logf = jnp.minimum(z, 0.0) - jnp.log1p(u)
    return logf, jnp.where(z >= 0, small, big), jnp.where(z >= 0, big, small)


def head_norm(o, gain):
    return (o * lax.rsqrt(jnp.mean(o * o, axis=-1, keepdims=True) + EPS) * gain).astype(BF)


def mix_kernel(heads, plen, lengths, x_ref, d_ref, wf_ref, wo_ref, bias_ref, gain_ref, sums_ref, dst_ref, gu_ref, down_ref,
               out_ref, dout_ref, states_ref, next_ref, gu_out, down_out,
               wf, wo, state, ws_s, ws_r, own_s, full, dfull, *rest):
    ex = Exchange(x_ref, d_ref, full, dfull, rest[:5], rest[5:10], rest[10], rest[11:], extra_peers=True)
    n_mlp, feat = full.shape[0], full.shape[2]
    per = wf_ref.shape[0] // feat
    dk = dst_ref.shape[-1]
    decodes = dst_ref.shape[0]
    req = ex.req

    def w_copy(i, o, mine):
        peer = lax.rem(req + o, ex.n_req)
        owner = req if mine else peer
        if i == 0:
            src = dst = wf.at[owner]
        elif i == 1:
            src = dst = wo.at[pl.ds(owner * per, per)]
        elif i == 2:
            src, dst = gu_ref, gu_out.at[owner]
        else:
            src, dst = down_ref, down_out.at[pl.ds(owner * per, per)]
        return ex.remote(src, dst, ws_s.at[i, o], ws_r.at[i, owner], (peer, ex.me))

    def own_copies():
        return (pltpu.make_async_copy(gu_ref, gu_out.at[req], own_s.at[0]),
                pltpu.make_async_copy(down_ref, down_out.at[pl.ds(req * per, per)], own_s.at[1]))

    def before():
        wf[req] = wf_ref[...].astype(BF)
        for p in range(per):
            wo[req * per + p] = wo_ref[:, p * feat:(p + 1) * feat].astype(BF)
        for i in range(2):
            for o in range(1, ex.n_req):
                w_copy(i, o, True).start()

    def mixing(block):
        acc = None
        for s in range(n_mlp):
            term = dot(block(s), wf[s // per, (s % per) * feat:(s % per + 1) * feat, :])
            acc = term if acc is None else acc + term
        return acc

    def step(m, k, sub):
        p = (k * CHUNK) // plen
        row0 = lax.rem(k * CHUNK, plen) + sub * SUB
        row = row0 + lax.broadcasted_iota(jnp.int32, (SUB, dk), 0)
        alive = row < lengths[p]
        lg, kg = [], []
        for h in range(heads):
            z = m[:, h * 3 * dk:h * 3 * dk + dk] + bias_ref[:, h * dk:(h + 1) * dk]
            logf, key, _ = gates(z)
            lg.append(jnp.where(alive, logf, 0.0))
            kg.append(jnp.where(alive, key, 0.0))
        lf = jnp.concatenate(lg, axis=1) if heads > 1 else lg[0]
        hi = lf.astype(BF)
        lo = (lf - hi.astype(F32)).astype(BF)
        decays = jnp.exp(dot(sums_ref[...], jnp.concatenate([hi, lo], axis=0)))
        t = lax.broadcasted_iota(jnp.int32, (SUB, SUB), 0)
        s = lax.broadcasted_iota(jnp.int32, (SUB, SUB), 1)
        outs = []
        for h in range(heads):
            cols = slice(h * dk, (h + 1) * dk)
            v = m[:, h * 3 * dk + dk:h * 3 * dk + 2 * dk]
            q = m[:, h * 3 * dk + 2 * dk:h * 3 * dk + 3 * dk]
            k_ = kg[h]
            v16 = v.astype(BF)
            head = decays[0:SUB, cols]
            tail = decays[SUB:2 * SUB, cols]
            old = jnp.where(row0 == 0, 0.0, state[h])
            o = dot((q * head).astype(BF), old.astype(BF), ((1,), (1,)))
            scores = None
            for level in range(LEVELS, 0, -1):
                e = decays[(level + 1) * SUB:(level + 2) * SUB, cols]
                right = (lax.broadcasted_iota(jnp.int32, (SUB, dk), 0) >> (level - 1)) & 1
                qt = jnp.where(right == 1, q * e, 0.0).astype(BF)
                kt = jnp.where(right == 1, 0.0, k_ * e).astype(BF)
                term = dot(qt, kt, ((1,), (1,)))
                if level == LEVELS:
                    scores = term
                else:
                    scores = scores + jnp.where((t >> level) == (s >> level), term, 0.0)
            o = o + dot(scores.astype(BF), v16)
            o = o + jnp.sum(q * k_, axis=-1, keepdims=True) * v
            outs.append(jnp.where(alive, o, 0.0))
            new = old * head[SUB - 1:SUB, :] + dot(v16, (k_ * tail).astype(BF), ((0,), (0,)))
            state[h] = new
            states_ref[p, h] = new.T
        return outs

    def normed(outs):
        rows = [head_norm(o, gain_ref[:, h * dk:(h + 1) * dk]) for h, o in enumerate(outs)]
        return jnp.concatenate(rows, axis=1) if heads > 1 else rows[0]

    def decode(m):
        outs = []
        pad = jnp.zeros((dk - DEC, dk), F32)
        for h in range(heads):
            z = m[:, h * 3 * dk:h * 3 * dk + dk] + bias_ref[:, h * dk:(h + 1) * dk]
            _, key, f = gates(z)
            v = m[:, h * 3 * dk + dk:h * 3 * dk + 2 * dk]
            q = m[:, h * 3 * dk + 2 * dk:h * 3 * dk + 3 * dk]
            f_t = jnp.concatenate([f, pad], axis=0).T
            k_t = jnp.concatenate([key, pad], axis=0).T
            q_t = jnp.concatenate([q, pad], axis=0).T
            rows = []
            for n in range(decodes):
                new = f_t[:, n:n + 1] * dst_ref[n, h] + k_t[:, n:n + 1] * v[n:n + 1, :]
                next_ref[n, h] = new
                rows.append(jnp.sum(q_t[:, n:n + 1] * new, axis=0, keepdims=True))
            rows.append(jnp.zeros((DEC - decodes, dk), F32))
            outs.append(jnp.concatenate(rows, axis=0))
        return normed(outs)

    def work(k, dec):
        if dec:
            m = mixing(lambda s: dfull[s])
            ex.share(k, decode(m), wo, True)
            return

        @pl.when(k == 0)
        def _():
            for o in range(1, ex.n_req):
                for i in range(2):
                    w_copy(i, o, False).wait_recv()
            for i in range(2, 4):
                for o in range(1, ex.n_req):
                    w_copy(i, o, True).start()
            for copy in own_copies():
                copy.start()
        m = mixing(lambda s: full[s, ex.rows(k), :])
        pieces = [normed(step(m[i * SUB:(i + 1) * SUB], k, i)) for i in range(CHUNK // SUB)]
        ex.share(k, jnp.concatenate(pieces, axis=0), wo)

    ex.run(work, out_ref, dout_ref, before)
    for o in range(1, ex.n_req):
        for i in range(4):
            w_copy(i, o, True).wait_send()
        for i in range(2, 4):
            w_copy(i, o, False).wait_recv()
    for copy in own_copies():
        copy.wait()


def mlp_kernel(x_ref, d_ref, gain_ref, wgu, wd, out_ref, dout_ref, full, dfull, *rest):
    ex = Exchange(x_ref, d_ref, full, dfull, rest[:5], rest[5:10], rest[10], rest[11:])
    n_mlp, feat = full.shape[0], full.shape[2]
    per = wgu.shape[2] // feat
    width = n_mlp * feat

    def work(k, dec):
        def block(s):
            return (dfull[s] if dec else full[s, ex.rows(k), :]).astype(F32)
        total = None
        for s in range(n_mlp):
            x = block(s)
            part = jnp.sum(x * x, axis=-1, keepdims=True)
            total = part if total is None else total + part
        scale = lax.rsqrt(total / width + EPS)
        gate = up = None
        for s in range(n_mlp):
            x = (block(s) * scale * gain_ref[:, s * feat:(s + 1) * feat]).astype(BF)
            part = slice((s % per) * feat, (s % per + 1) * feat)
            g = dot(x, wgu[s // per, 0, part, :])
            u = dot(x, wgu[s // per, 1, part, :])
            gate = g if gate is None else gate + g
            up = u if up is None else up + u
        hidden = (gate / (1.0 + jnp.exp(-gate)) * up).astype(BF)
        ex.share(k, hidden, wd, dec)

    ex.run(work, out_ref, dout_ref)


def exchange_scratch(n_mlp, count, feat):
    chips = n_mlp // 2
    dma = pltpu.SemaphoreType.DMA
    big = pltpu.VMEM((count, chips, CHUNK, feat), BF)
    small = pltpu.VMEM((chips, DEC, feat), BF)
    return [
        pltpu.VMEM((n_mlp, count * CHUNK, feat), BF),
        pltpu.VMEM((n_mlp, DEC, feat), BF),
        big, big, big, pltpu.VMEM((count, chips + 1, CHUNK, feat), BF), pltpu.VMEM((2, chips, CHUNK, feat), F32),
        small, small, small, small, pltpu.VMEM((chips, DEC, feat), F32),
        pltpu.VMEM((CHUNK, feat), F32),
        dma((count, chips + 1)), dma((count, chips)), dma((count, n_mlp)),
        dma((chips,)), dma((chips,)), dma((n_mlp,)),
        dma((count + 1,)), dma((count + 1,)), dma((count, chips)), dma((count, chips + 1)),
        dma((chips,)), dma((chips,)),
    ]


def on_device(n_req, n_mlp, prompt_tokens, decode_tokens, prompt_lengths, decode_states, w_fio, forget_bias,
              head_gain, w_out, mlp_gain, w_gu, w_down):
    prompts, plen, feat = prompt_tokens.shape
    decodes, heads, dk, _ = decode_states.shape
    rows = prompts * plen
    count = rows // CHUNK
    per = w_fio.shape[0] // feat
    vmem = pl.BlockSpec(memory_space=pltpu.VMEM)
    anywhere = pl.BlockSpec(memory_space=pl.ANY)
    x = prompt_tokens.reshape(rows, feat)
    d = jnp.pad(decode_tokens, ((0, DEC - decodes), (0, 0)))
    params = functools.partial(pltpu.CompilerParams, has_side_effects=True, vmem_limit_bytes=58 * 2**20)
    hidden = w_down.shape[0]

    gu = w_gu.astype(BF).reshape(w_gu.shape[0], 2, hidden).transpose(1, 0, 2)
    down = w_down.astype(BF).reshape(hidden, per, feat).transpose(1, 0, 2)

    dma = pltpu.SemaphoreType.DMA
    residual, dresidual, states, after, gu, down = pl.pallas_call(
        functools.partial(mix_kernel, heads, plen),
        out_shape=(
            jax.ShapeDtypeStruct((rows, feat), BF),
            jax.ShapeDtypeStruct((DEC, feat), BF),
            jax.ShapeDtypeStruct((prompts, heads, dk, dk), F32),
            jax.ShapeDtypeStruct((decodes, heads, dk, dk), F32),
            jax.ShapeDtypeStruct((n_req,) + gu.shape, BF),
            jax.ShapeDtypeStruct((n_mlp,) + down.shape[1:], BF),
        ),
        in_specs=[pl.BlockSpec(memory_space=pltpu.SMEM)] + [vmem] * 8 + [anywhere] * 2,
        out_specs=(vmem,) * 4 + (anywhere,) * 2,
        scratch_shapes=[
            pltpu.VMEM((n_req,) + w_fio.shape, BF),
            pltpu.VMEM((n_mlp, heads * dk, feat), BF),
            pltpu.VMEM((heads, dk, dk), F32),
            dma((4, n_req)), dma((4, n_req)), dma((2,)),
        ] + exchange_scratch(n_mlp, count, feat),
        compiler_params=params(collective_id=0),
        name="mix",
    )(prompt_lengths, x, d, w_fio, w_out, forget_bias.reshape(1, -1), head_gain.reshape(1, -1),
      jnp.asarray(decay_sums(), BF), decode_states, gu, down)

    out, dout = pl.pallas_call(
        mlp_kernel,
        out_shape=(jax.ShapeDtypeStruct((rows, feat), BF), jax.ShapeDtypeStruct((DEC, feat), BF)),
        in_specs=[vmem] * 5,
        out_specs=(vmem,) * 2,
        scratch_shapes=exchange_scratch(n_mlp, count, feat),
        compiler_params=params(collective_id=1),
        name="mlp",
    )(residual, dresidual, mlp_gain.reshape(1, -1), gu, down)
    return out.reshape(prompts, plen, feat), dout[:decodes], states, after


def solution(mesh):
    placed = (
        P("req", None, "mlp"),
        P("req", "mlp"),
        P("req"),
        P("req", "mlp", None, None),
        P("req", "mlp"),
        P("mlp"),
        P("mlp"),
        P("mlp", "req"),
        P(),
        P("req", "mlp"),
        P("mlp", "req"),
    )
    return jax.shard_map(
        functools.partial(on_device, mesh.shape["req"], mesh.shape["mlp"]),
        mesh=mesh,
        in_specs=placed,
        out_specs=(
            P("req", None, "mlp"),
            P("req", "mlp"),
            P("req", "mlp", None, None),
            P("req", "mlp", None, None),
        ),
        check_vma=False,
    )
```

```python
import functools

import jax
import jax.numpy as jnp
import numpy as np
from jax import lax
from jax.experimental import pallas as pl
from jax.experimental.pallas import tpu as pltpu
from jax.sharding import PartitionSpec as P

MESH = pl.DeviceIdType.MESH
EPS = 1e-05
SUB = 128
LEVELS = 7
CHUNK = 128
DEC = 16
BF = jnp.bfloat16
F32 = jnp.float32


def decay_sums():
    t = np.arange(SUB)[:, None]
    s = np.arange(SUB)[None, :]
    parts = [s <= t, s > t]
    for level in range(1, LEVELS + 1):
        block = 1 << level
        middle = (t // block) * block + block // 2 - 1
        parts.append(((s > middle) & (s <= t)) | ((s > t) & (s <= middle)))
    stacked = np.concatenate(parts, axis=0).astype(np.float32)
    return np.concatenate([stacked, stacked], axis=1)


def dot(a, b, dims=((1,), (0,))):
    return lax.dot_general(a, b, (dims, ((), ())), preferred_element_type=F32)


class Exchange:
    def __init__(self, x_ref, d_ref, full, dfull, bufs, dbufs, tot, sems, extra_peers=False):
        self.req = lax.axis_index("req")
        self.me = lax.axis_index("mlp")
        self.n_req = lax.axis_size("req")
        self.chips = lax.axis_size("mlp") // 2
        self.chip = self.me // 2
        self.core = self.me % 2
        self.x, self.d = x_ref, d_ref
        self.full, self.dfull = full, dfull
        self.sib_out, self.sib_in, self.sums, self.z_in, self.keep = bufs
        self.dbufs = dbufs
        self.tot = tot
        (self.line_s, self.pair_s, self.got, self.dga_s, self.dgr_s, self.dgot,
         self.sb_s, self.sb_r, self.z_s, self.z_r, self.dz_s, self.dz_r) = sems
        self.extra = extra_peers
        self.count = x_ref.shape[0] // CHUNK

    def sibling(self):
        return (self.req, self.chip * 2 + 1 - self.core)

    def far(self, o):
        j = lax.rem(self.chip + o, self.chips)
        return j, (self.req, j * 2 + self.core)

    def beside(self, right):
        j = self.chip + (1 if right else -1)
        return (self.req, j * 2 + self.core)

    def enter(self):
        barrier = pltpu.get_barrier_semaphore()
        peers = [self.sibling()] + [self.far(o)[1] for o in range(1, self.chips)]
        if self.extra:
            peers += [(lax.rem(self.req + o, self.n_req), self.me) for o in range(1, self.n_req)]
        for peer in peers:
            pl.semaphore_signal(barrier, inc=1, device_id=peer, device_id_type=MESH)
        pl.semaphore_wait(barrier, len(peers))

    def rows(self, k):
        return pl.ds(pl.multiple_of(k * CHUNK, CHUNK), CHUNK)

    def remote(self, src, dst, ssem, rsem, dev):
        return pltpu.make_async_remote_copy(
            src_ref=src, dst_ref=dst, send_sem=ssem, recv_sem=rsem, device_id=dev, device_id_type=MESH)


    def has(self, right):
        return self.chip + 1 < self.chips if right else self.chip > 0

    def block_copy(self, k, h, from_left, to):
        src_chip = self.chip - h if from_left else self.chip + h
        source = src_chip * 2 + self.core
        slot = self.full.at[source, self.rows(k)]
        src = slot if h else self.x.at[self.rows(k)]
        if to == "line":
            sem = self.line_s.at[k, self.chips if h == 0 and not from_left else src_chip]
            dev = self.beside(from_left)
        else:
            sem, dev = self.pair_s.at[k, src_chip], self.sibling()
        return self.remote(src, slot, sem, self.got.at[k, source], dev)

    def each_send(self, k, h, act):
        for from_left in (True, False):
            there = self.chip - h >= 0 if from_left else self.chip + h < self.chips

            def go(from_left=from_left):
                if h and act == "start":
                    source = (self.chip - h if from_left else self.chip + h) * 2 + self.core
                    slot = self.full.at[source, self.rows(k)]
                    self.remote(slot, slot, self.pair_s.at[k, 0], self.got.at[k, source], self.sibling()).wait_recv()

                @pl.when(self.has(from_left))
                def _():
                    copy = self.block_copy(k, h, from_left, "line")
                    copy.start() if act == "start" else copy.wait_send()
                if h or from_left:
                    copy = self.block_copy(k, h, from_left, "pair")
                    copy.start() if act == "start" else copy.wait_send()
            if h:
                pl.when(there)(go)
            else:
                go()

    def hop(self, k, h):
        self.each_send(k, h, "start")
        if h == 0:
            self.full[self.me, self.rows(k), :] = self.x[self.rows(k), :]

    def gather_done(self, k):
        for j in range(self.chips):
            source = j * 2 + 1 - self.core
            slot = self.full.at[source, self.rows(k)]
            self.remote(slot, slot, self.pair_s.at[k, 0], self.got.at[k, source], self.sibling()).wait_recv()


    def dgather_copy(self, o):
        dev = self.sibling() if o == 0 else self.far(o)[1]
        return self.remote(self.d, self.dfull.at[self.me], self.dga_s.at[o], self.dgot.at[self.me], dev)

    def drelay_copy(self, o):
        src = self.far(o)[0] * 2 + self.core
        return self.remote(self.dfull.at[src], self.dfull.at[src], self.dgr_s.at[o], self.dgot.at[src], self.sibling())

    def darrive(self, src):
        slot = self.dfull.at[src]
        self.remote(slot, slot, self.dgr_s.at[0], self.dgot.at[src], self.sibling()).wait_recv()

    def dgather_start(self):
        for o in range(self.chips):
            self.dgather_copy(o).start()
        self.dfull[self.me] = self.d[...]

    def drelay(self):
        for o in range(1, self.chips):
            self.darrive(self.far(o)[0] * 2 + self.core)
            self.drelay_copy(o).start()

    def dgather_done(self):
        for j in range(self.chips):
            self.darrive(j * 2 + 1 - self.core)


    def sib_copy(self, k, dec):
        src, dst = self.dbufs[:2] if dec else (self.sib_out.at[k], self.sib_in.at[k])
        return self.remote(src, dst, self.sb_s.at[k], self.sb_r.at[k], self.sibling())

    def share(self, k, operand, weights, dec=False):
        par = lax.rem(k, 2)
        for j in range(self.chips):
            term = dot(operand, weights[j * 2 + 1 - self.core]).astype(BF)
            if dec:
                self.dbufs[0][j] = term
            else:
                self.sib_out[k, j] = term
        self.sib_copy(k, dec).start()
        for j in range(self.chips):
            term = dot(operand, weights[j * 2 + self.core])
            if dec:
                self.dbufs[4][j] = term
            else:
                self.keep[par, j] = term

    def pair_sum(self, k):
        par = lax.rem(k, 2)
        self.sib_copy(k, False).wait_recv()
        for j in range(self.chips):
            self.sums[k, j] = (self.keep[par, j] + self.sib_in[k, j].astype(F32)).astype(BF)

    def sum_copy(self, k, j, right):
        place = j if right else jnp.where(self.chip - 1 == j, self.chips, j)
        return self.remote(self.sums.at[k, j], self.z_in.at[k, place], self.z_s.at[k, j], self.z_r.at[k, place],
                           self.beside(right))

    def sum_wait(self, k, place):
        ref = self.z_in.at[k, place]
        self.remote(ref, ref, self.z_s.at[k, 0], self.z_r.at[k, place], self.sibling()).wait_recv()

    def chain(self, k, right):
        for j in range(self.chips):
            @pl.when(self.chip < j if right else self.chip > j)
            def _():
                @pl.when(self.has(not right))
                def _():
                    self.sum_wait(k, j)
                    self.sums[k, j] = (self.sums[k, j].astype(F32) + self.z_in[k, j].astype(F32)).astype(BF)
                self.sum_copy(k, j, right).start()

    def total(self, k, out_ref):
        self.tot[...] = self.x[self.rows(k), :].astype(F32) + self.sums[k, self.chip].astype(F32)
        for right, place in ((False, self.chip), (True, self.chips)):
            @pl.when(self.has(right))
            def _():
                self.sum_wait(k, place)
                self.tot[...] += self.z_in[k, place].astype(F32)
        out_ref[self.rows(k), :] = self.tot[...].astype(BF)

    def dz_copy(self, o):
        j, dev = self.far(o)
        return self.remote(self.dbufs[2].at[j], self.dbufs[3].at[self.chip], self.dz_s.at[o],
                           self.dz_r.at[self.chip], dev)

    def dpair_sum(self):
        b = self.dbufs
        self.sib_copy(self.count, True).wait_recv()
        for o in list(range(1, self.chips)) + [0]:
            j = self.far(o)[0]
            b[2][j] = (b[4][j] + b[1][j].astype(F32)).astype(BF)
            if o:
                self.dz_copy(o).start()

    def dtotal(self, out_ref):
        b = self.dbufs
        acc = self.d[...].astype(F32) + b[2][self.chip].astype(F32)
        for o in range(1, self.chips):
            j, dev = self.far(o)
            ref = b[3].at[j]
            self.remote(ref, ref, self.dz_s.at[o], self.dz_r.at[j], dev).wait_recv()
            acc = acc + b[3][j].astype(F32)
        out_ref[...] = acc.astype(BF)
        for o in range(self.chips):
            self.dgather_copy(o).wait_send()
        for o in range(1, self.chips):
            self.drelay_copy(o).wait_send()
            self.dz_copy(o).wait_send()
        self.sib_copy(self.count, True).wait_send()

    def finish(self, k):
        for h in range(self.chips):
            self.each_send(k, h, "wait")
        self.sib_copy(k, False).wait_send()
        for j in range(self.chips):
            for right in (True, False):
                @pl.when(self.chip < j if right else self.chip > j)
                def _():
                    self.sum_copy(k, j, right).wait_send()

    def run(self, work, out_ref, dout_ref, lead, before=None, hooks=()):
        count, chips = self.count, self.chips

        def at(k, action):
            @pl.when((k >= 0) & (k < count))
            def _():
                action(k)

        self.enter()
        if before is not None:
            before()
        self.dgather_start()

        def body(step, c):
            i = step - lead
            for h in range(chips):
                at(i + lead - h, functools.partial(self.hop, h=h))
            for when, action in hooks:
                pl.when(i == when)(action)
            pl.when(i == 1)(self.drelay)

            def compute(k):
                self.gather_done(k)
                work(k, False)
            at(i, compute)

            @pl.when(i == 2)
            def _():
                self.dgather_done()
                work(count, True)
            pl.when(i == 3)(self.dpair_sum)
            at(i - 1, self.pair_sum)
            at(i - 1 - self.chip, functools.partial(self.chain, right=True))
            at(i - chips + self.chip, functools.partial(self.chain, right=False))
            at(i - chips - 1, functools.partial(self.total, out_ref=out_ref))
            return c

        lax.fori_loop(0, count + lead + chips + 1, body, 0)
        self.dtotal(dout_ref)
        lax.fori_loop(0, count, lambda k, c: (self.finish(k), c)[1], 0)


def gates(z):
    u = jnp.exp(-jnp.abs(z))
    big = 1.0 / (1.0 + u)
    small = u * big
    logf = jnp.minimum(z, 0.0) - jnp.log1p(u)
    return logf, jnp.where(z >= 0, small, big), jnp.where(z >= 0, big, small)


def head_norm(o, gain):
    return (o * lax.rsqrt(jnp.mean(o * o, axis=-1, keepdims=True) + EPS) * gain).astype(BF)


def mix_kernel(heads, plen, lengths, x_ref, d_ref, wf_ref, wo_ref, bias_ref, gain_ref, sums_ref, dst_ref, gu_ref, down_ref,
               out_ref, dout_ref, states_ref, next_ref, gu_out, down_out,
               wf, wo, state, ws_s, ws_r, own_s, full, dfull, *rest):
    ex = Exchange(x_ref, d_ref, full, dfull, rest[:5], rest[5:10], rest[10], rest[11:], extra_peers=True)
    n_mlp, feat = full.shape[0], full.shape[2]
    per = wf_ref.shape[0] // feat
    dk = dst_ref.shape[-1]
    decodes = dst_ref.shape[0]
    req = ex.req

    square = ex.n_req == 4
    if square:
        x_peer = req + 1 - 2 * (req % 2)
        y_peer = lax.rem(req + 2, 4)
        cross = lax.rem(x_peer + 2, 4)
        ways, relays = (0, 1), (2, 3)
        targets = (x_peer, y_peer, y_peer, x_peer)
    else:
        ways, relays = tuple(range(1, ex.n_req)), ()

    def place(i, owner, half=None):
        buf = (wf, wo, gu_out, down_out)[i]
        rows = slice(None)
        if half is not None:
            n = buf.shape[2 if i == 2 else 1] // 2
            rows = pl.ds(half * n, n)
        if i == 0:
            return buf.at[owner, rows]
        if i == 2:
            return buf.at[owner, :, rows]
        return buf.at[pl.ds(owner * per, per), rows]

    def w_send(i, way):
        if way in relays:
            ref = place(i, (x_peer, y_peer)[way - 2], way - 2)
            return ex.remote(ref, ref, ws_s.at[i, way], ws_r.at[i, way], (targets[way], ex.me))
        src = gu_ref if i == 2 else down_ref if i == 3 else place(i, req)
        peer = targets[way] if square else lax.rem(req + way, ex.n_req)
        at = way if square else req
        return ex.remote(src, place(i, req), ws_s.at[i, way], ws_r.at[i, at], (peer, ex.me))

    def w_wait(i, way):
        if way in relays:
            ref, at = place(i, cross, way - 2), way
        elif square:
            ref, at = place(i, targets[way]), way
        else:
            at = lax.rem(req + way, ex.n_req)
            ref = place(i, at)
        peer = lax.rem(req + 1, ex.n_req)
        ex.remote(ref, ref, ws_s.at[i, way], ws_r.at[i, at], (peer, ex.me)).wait_recv()

    def w_all(items, which, act):
        for i in items:
            for way in which:
                if act == "start":
                    w_send(i, way).start()
                elif act == "sent":
                    w_send(i, way).wait_send()
                else:
                    w_wait(i, way)

    def own_copies():
        return (pltpu.make_async_copy(gu_ref, gu_out.at[req], own_s.at[0]),
                pltpu.make_async_copy(down_ref, down_out.at[pl.ds(req * per, per)], own_s.at[1]))

    def before():
        wf[req] = wf_ref[...].astype(BF)
        for p in range(per):
            wo[req * per + p] = wo_ref[:, p * feat:(p + 1) * feat].astype(BF)
        w_all((0, 1), ways, "start")

    def first_relay():
        w_all((0, 1), ways, "wait")
        w_all((0, 1), relays, "start")
        w_all((2, 3), ways, "start")
        for copy in own_copies():
            copy.start()

    def second_relay():
        w_all((2, 3), ways, "wait")
        w_all((2, 3), relays, "start")

    def mixing(block):
        acc = None
        for s in range(n_mlp):
            term = dot(block(s), wf[s // per, (s % per) * feat:(s % per + 1) * feat, :])
            acc = term if acc is None else acc + term
        return acc

    def step(m, k, sub):
        p = (k * CHUNK) // plen
        row0 = lax.rem(k * CHUNK, plen) + sub * SUB
        row = row0 + lax.broadcasted_iota(jnp.int32, (SUB, dk), 0)
        alive = row < lengths[p]
        lg, kg = [], []
        for h in range(heads):
            z = m[:, h * 3 * dk:h * 3 * dk + dk] + bias_ref[:, h * dk:(h + 1) * dk]
            logf, key, _ = gates(z)
            lg.append(jnp.where(alive, logf, 0.0))
            kg.append(jnp.where(alive, key, 0.0))
        lf = jnp.concatenate(lg, axis=1) if heads > 1 else lg[0]
        hi = lf.astype(BF)
        lo = (lf - hi.astype(F32)).astype(BF)
        decays = jnp.exp(dot(sums_ref[...], jnp.concatenate([hi, lo], axis=0)))
        t = lax.broadcasted_iota(jnp.int32, (SUB, SUB), 0)
        s = lax.broadcasted_iota(jnp.int32, (SUB, SUB), 1)
        outs = []
        for h in range(heads):
            cols = slice(h * dk, (h + 1) * dk)
            v = m[:, h * 3 * dk + dk:h * 3 * dk + 2 * dk]
            q = m[:, h * 3 * dk + 2 * dk:h * 3 * dk + 3 * dk]
            k_ = kg[h]
            v16 = v.astype(BF)
            head = decays[0:SUB, cols]
            tail = decays[SUB:2 * SUB, cols]
            old = jnp.where(row0 == 0, 0.0, state[h])
            o = dot((q * head).astype(BF), old.astype(BF), ((1,), (1,)))
            scores = None
            for level in range(LEVELS, 0, -1):
                e = decays[(level + 1) * SUB:(level + 2) * SUB, cols]
                right = (lax.broadcasted_iota(jnp.int32, (SUB, dk), 0) >> (level - 1)) & 1
                qt = jnp.where(right == 1, q * e, 0.0).astype(BF)
                kt = jnp.where(right == 1, 0.0, k_ * e).astype(BF)
                term = dot(qt, kt, ((1,), (1,)))
                if level == LEVELS:
                    scores = term
                else:
                    scores = scores + jnp.where((t >> level) == (s >> level), term, 0.0)
            o = o + dot(scores.astype(BF), v16)
            o = o + jnp.sum(q * k_, axis=-1, keepdims=True) * v
            outs.append(jnp.where(alive, o, 0.0))
            new = old * head[SUB - 1:SUB, :] + dot(v16, (k_ * tail).astype(BF), ((0,), (0,)))
            state[h] = new
            states_ref[p, h] = new.T
        return outs

    def normed(outs):
        rows = [head_norm(o, gain_ref[:, h * dk:(h + 1) * dk]) for h, o in enumerate(outs)]
        return jnp.concatenate(rows, axis=1) if heads > 1 else rows[0]

    def decode(m):
        outs = []
        pad = jnp.zeros((dk - DEC, dk), F32)
        for h in range(heads):
            z = m[:, h * 3 * dk:h * 3 * dk + dk] + bias_ref[:, h * dk:(h + 1) * dk]
            _, key, f = gates(z)
            v = m[:, h * 3 * dk + dk:h * 3 * dk + 2 * dk]
            q = m[:, h * 3 * dk + 2 * dk:h * 3 * dk + 3 * dk]
            f_t = jnp.concatenate([f, pad], axis=0).T
            k_t = jnp.concatenate([key, pad], axis=0).T
            q_t = jnp.concatenate([q, pad], axis=0).T
            rows = []
            for n in range(decodes):
                new = f_t[:, n:n + 1] * dst_ref[n, h] + k_t[:, n:n + 1] * v[n:n + 1, :]
                next_ref[n, h] = new
                rows.append(jnp.sum(q_t[:, n:n + 1] * new, axis=0, keepdims=True))
            rows.append(jnp.zeros((DEC - decodes, dk), F32))
            outs.append(jnp.concatenate(rows, axis=0))
        return normed(outs)

    def work(k, dec):
        if dec:
            m = mixing(lambda s: dfull[s])
            ex.share(k, decode(m), wo, True)
            return

        @pl.when(k == 0)
        def _():
            w_all((0, 1), relays, "wait")
        m = mixing(lambda s: full[s, ex.rows(k), :])
        pieces = [normed(step(m[i * SUB:(i + 1) * SUB], k, i)) for i in range(CHUNK // SUB)]
        ex.share(k, jnp.concatenate(pieces, axis=0), wo)

    lead = max(ex.chips, ex.count * 3 // 4)
    ex.run(work, out_ref, dout_ref, lead, before, ((lead // 2 - lead, first_relay), (ex.count // 2, second_relay)))
    w_all((2, 3), relays, "wait")
    for i in range(4):
        w_all((i,), ways + relays, "sent")
    for copy in own_copies():
        copy.wait()


def mlp_kernel(x_ref, d_ref, gain_ref, wgu, wd, out_ref, dout_ref, full, dfull, *rest):
    ex = Exchange(x_ref, d_ref, full, dfull, rest[:5], rest[5:10], rest[10], rest[11:])
    n_mlp, feat = full.shape[0], full.shape[2]
    per = wgu.shape[2] // feat
    width = n_mlp * feat

    def work(k, dec):
        def block(s):
            return (dfull[s] if dec else full[s, ex.rows(k), :]).astype(F32)
        total = None
        for s in range(n_mlp):
            x = block(s)
            part = jnp.sum(x * x, axis=-1, keepdims=True)
            total = part if total is None else total + part
        scale = lax.rsqrt(total / width + EPS)
        gate = up = None
        for s in range(n_mlp):
            x = (block(s) * scale * gain_ref[:, s * feat:(s + 1) * feat]).astype(BF)
            part = slice((s % per) * feat, (s % per + 1) * feat)
            g = dot(x, wgu[s // per, 0, part, :])
            u = dot(x, wgu[s // per, 1, part, :])
            gate = g if gate is None else gate + g
            up = u if up is None else up + u
        hidden = (gate / (1.0 + jnp.exp(-gate)) * up).astype(BF)
        ex.share(k, hidden, wd, dec)

    ex.run(work, out_ref, dout_ref, ex.chips)


def exchange_scratch(n_mlp, count, feat):
    chips = n_mlp // 2
    dma = pltpu.SemaphoreType.DMA
    big = pltpu.VMEM((count, chips, CHUNK, feat), BF)
    small = pltpu.VMEM((chips, DEC, feat), BF)
    return [
        pltpu.VMEM((n_mlp, count * CHUNK, feat), BF),
        pltpu.VMEM((n_mlp, DEC, feat), BF),
        big, big, big, pltpu.VMEM((count, chips + 1, CHUNK, feat), BF), pltpu.VMEM((2, chips, CHUNK, feat), F32),
        small, small, small, small, pltpu.VMEM((chips, DEC, feat), F32),
        pltpu.VMEM((CHUNK, feat), F32),
        dma((count, chips + 1)), dma((count, chips)), dma((count, n_mlp)),
        dma((chips,)), dma((chips,)), dma((n_mlp,)),
        dma((count + 1,)), dma((count + 1,)), dma((count, chips)), dma((count, chips + 1)),
        dma((chips,)), dma((chips,)),
    ]


def on_device(n_req, n_mlp, prompt_tokens, decode_tokens, prompt_lengths, decode_states, w_fio, forget_bias,
              head_gain, w_out, mlp_gain, w_gu, w_down):
    prompts, plen, feat = prompt_tokens.shape
    decodes, heads, dk, _ = decode_states.shape
    rows = prompts * plen
    count = rows // CHUNK
    per = w_fio.shape[0] // feat
    vmem = pl.BlockSpec(memory_space=pltpu.VMEM)
    anywhere = pl.BlockSpec(memory_space=pl.ANY)
    x = prompt_tokens.reshape(rows, feat)
    d = jnp.pad(decode_tokens, ((0, DEC - decodes), (0, 0)))
    params = functools.partial(pltpu.CompilerParams, has_side_effects=True, vmem_limit_bytes=58 * 2**20)
    hidden = w_down.shape[0]

    gu = w_gu.astype(BF).reshape(w_gu.shape[0], 2, hidden).transpose(1, 0, 2)
    down = w_down.astype(BF).reshape(hidden, per, feat).transpose(1, 0, 2)

    dma = pltpu.SemaphoreType.DMA
    residual, dresidual, states, after, gu, down = pl.pallas_call(
        functools.partial(mix_kernel, heads, plen),
        out_shape=(
            jax.ShapeDtypeStruct((rows, feat), BF),
            jax.ShapeDtypeStruct((DEC, feat), BF),
            jax.ShapeDtypeStruct((prompts, heads, dk, dk), F32),
            jax.ShapeDtypeStruct((decodes, heads, dk, dk), F32),
            jax.ShapeDtypeStruct((n_req,) + gu.shape, BF),
            jax.ShapeDtypeStruct((n_mlp,) + down.shape[1:], BF),
        ),
        in_specs=[pl.BlockSpec(memory_space=pltpu.SMEM)] + [vmem] * 8 + [anywhere] * 2,
        out_specs=(vmem,) * 4 + (anywhere,) * 2,
        scratch_shapes=[
            pltpu.VMEM((n_req,) + w_fio.shape, BF),
            pltpu.VMEM((n_mlp, heads * dk, feat), BF),
            pltpu.VMEM((heads, dk, dk), F32),
            dma((4, n_req)), dma((4, n_req)), dma((2,)),
        ] + exchange_scratch(n_mlp, count, feat),
        compiler_params=params(collective_id=0),
        name="mix",
    )(prompt_lengths, x, d, w_fio, w_out, forget_bias.reshape(1, -1), head_gain.reshape(1, -1),
      jnp.asarray(decay_sums(), BF), decode_states, gu, down)

    out, dout = pl.pallas_call(
        mlp_kernel,
        out_shape=(jax.ShapeDtypeStruct((rows, feat), BF), jax.ShapeDtypeStruct((DEC, feat), BF)),
        in_specs=[vmem] * 5,
        out_specs=(vmem,) * 2,
        scratch_shapes=exchange_scratch(n_mlp, count, feat),
        compiler_params=params(collective_id=1),
        name="mlp",
    )(residual, dresidual, mlp_gain.reshape(1, -1), gu, down)
    return out.reshape(prompts, plen, feat), dout[:decodes], states, after


def solution(mesh):
    placed = (
        P("req", None, "mlp"),
        P("req", "mlp"),
        P("req"),
        P("req", "mlp", None, None),
        P("req", "mlp"),
        P("mlp"),
        P("mlp"),
        P("mlp", "req"),
        P(),
        P("req", "mlp"),
        P("mlp", "req"),
    )
    return jax.shard_map(
        functools.partial(on_device, mesh.shape["req"], mesh.shape["mlp"]),
        mesh=mesh,
        in_specs=placed,
        out_specs=(
            P("req", None, "mlp"),
            P("req", "mlp"),
            P("req", "mlp", None, None),
            P("req", "mlp", None, None),
        ),
        check_vma=False,
    )
```

```python
import functools

import jax
import jax.numpy as jnp
import numpy as np
from jax import lax
from jax.experimental import pallas as pl
from jax.experimental.pallas import tpu as pltpu
from jax.sharding import PartitionSpec as P

MESH = pl.DeviceIdType.MESH
EPS = 1e-05
SUB = 128
LEVELS = 7
CHUNK = 256
DEC = 16
BF = jnp.bfloat16
F32 = jnp.float32


def decay_sums():
    t = np.arange(SUB)[:, None]
    s = np.arange(SUB)[None, :]
    parts = [s <= t, s > t]
    for level in range(1, LEVELS + 1):
        block = 1 << level
        middle = (t // block) * block + block // 2 - 1
        parts.append(((s > middle) & (s <= t)) | ((s > t) & (s <= middle)))
    stacked = np.concatenate(parts, axis=0).astype(np.float32)
    return np.concatenate([stacked, stacked], axis=1)


def dot(a, b, dims=((1,), (0,))):
    return lax.dot_general(a, b, (dims, ((), ())), preferred_element_type=F32)


class Exchange:
    def __init__(self, x_ref, d_ref, full, dfull, bufs, dbufs, tot, sems, extra_peers=False):
        self.req = lax.axis_index("req")
        self.me = lax.axis_index("mlp")
        self.n_req = lax.axis_size("req")
        self.chips = lax.axis_size("mlp") // 2
        self.chip = self.me // 2
        self.core = self.me % 2
        self.x, self.d = x_ref, d_ref
        self.full, self.dfull = full, dfull
        self.sib_out, self.sib_in, self.sums, self.z_in, self.keep = bufs
        self.dbufs = dbufs
        self.tot = tot
        (self.line_s, self.pair_s, self.got, self.dga_s, self.dgr_s, self.dgot,
         self.sb_s, self.sb_r, self.z_s, self.z_r, self.dz_s, self.dz_r) = sems
        self.extra = extra_peers
        self.count = x_ref.shape[0] // CHUNK

    def sibling(self):
        return (self.req, self.chip * 2 + 1 - self.core)

    def far(self, o):
        j = lax.rem(self.chip + o, self.chips)
        return j, (self.req, j * 2 + self.core)

    def beside(self, right):
        j = self.chip + (1 if right else -1)
        return (self.req, j * 2 + self.core)

    def enter(self):
        barrier = pltpu.get_barrier_semaphore()
        peers = [self.sibling()] + [self.far(o)[1] for o in range(1, self.chips)]
        if self.extra:
            peers += [(lax.rem(self.req + o, self.n_req), self.me) for o in range(1, self.n_req)]
        for peer in peers:
            pl.semaphore_signal(barrier, inc=1, device_id=peer, device_id_type=MESH)
        pl.semaphore_wait(barrier, len(peers))

    def rows(self, k):
        return pl.ds(pl.multiple_of(k * CHUNK, CHUNK), CHUNK)

    def remote(self, src, dst, ssem, rsem, dev):
        return pltpu.make_async_remote_copy(
            src_ref=src, dst_ref=dst, send_sem=ssem, recv_sem=rsem, device_id=dev, device_id_type=MESH)


    def has(self, right):
        return self.chip + 1 < self.chips if right else self.chip > 0

    def block_copy(self, k, h, from_left, to):
        src_chip = self.chip - h if from_left else self.chip + h
        source = src_chip * 2 + self.core
        slot = self.full.at[source, self.rows(k)]
        src = slot if h else self.x.at[self.rows(k)]
        if to == "line":
            sem = self.line_s.at[k, self.chips if h == 0 and not from_left else src_chip]
            dev = self.beside(from_left)
        else:
            sem, dev = self.pair_s.at[k, src_chip], self.sibling()
        return self.remote(src, slot, sem, self.got.at[k, source], dev)

    def each_send(self, k, h, act):
        for from_left in (True, False):
            there = self.chip - h >= 0 if from_left else self.chip + h < self.chips

            def go(from_left=from_left):
                if h and act == "start":
                    source = (self.chip - h if from_left else self.chip + h) * 2 + self.core
                    slot = self.full.at[source, self.rows(k)]
                    self.remote(slot, slot, self.pair_s.at[k, 0], self.got.at[k, source], self.sibling()).wait_recv()

                @pl.when(self.has(from_left))
                def _():
                    copy = self.block_copy(k, h, from_left, "line")
                    copy.start() if act == "start" else copy.wait_send()
                if h or from_left:
                    copy = self.block_copy(k, h, from_left, "pair")
                    copy.start() if act == "start" else copy.wait_send()
            if h:
                pl.when(there)(go)
            else:
                go()

    def hop(self, k, h):
        self.each_send(k, h, "start")
        if h == 0:
            self.full[self.me, self.rows(k), :] = self.x[self.rows(k), :]

    def gather_done(self, k):
        for j in range(self.chips):
            source = j * 2 + 1 - self.core
            slot = self.full.at[source, self.rows(k)]
            self.remote(slot, slot, self.pair_s.at[k, 0], self.got.at[k, source], self.sibling()).wait_recv()


    def dgather_copy(self, o):
        dev = self.sibling() if o == 0 else self.far(o)[1]
        return self.remote(self.d, self.dfull.at[self.me], self.dga_s.at[o], self.dgot.at[self.me], dev)

    def drelay_copy(self, o):
        src = self.far(o)[0] * 2 + self.core
        return self.remote(self.dfull.at[src], self.dfull.at[src], self.dgr_s.at[o], self.dgot.at[src], self.sibling())

    def darrive(self, src):
        slot = self.dfull.at[src]
        self.remote(slot, slot, self.dgr_s.at[0], self.dgot.at[src], self.sibling()).wait_recv()

    def dgather_start(self):
        for o in range(self.chips):
            self.dgather_copy(o).start()
        self.dfull[self.me] = self.d[...]

    def drelay(self):
        for o in range(1, self.chips):
            self.darrive(self.far(o)[0] * 2 + self.core)
            self.drelay_copy(o).start()

    def dgather_done(self):
        for j in range(self.chips):
            self.darrive(j * 2 + 1 - self.core)


    def sib_copy(self, k, dec):
        src, dst = self.dbufs[:2] if dec else (self.sib_out.at[k], self.sib_in.at[k])
        return self.remote(src, dst, self.sb_s.at[k], self.sb_r.at[k], self.sibling())

    def share(self, k, operand, weights, dec=False):
        par = lax.rem(k, 2)
        for j in range(self.chips):
            term = dot(operand, weights[j * 2 + 1 - self.core]).astype(BF)
            if dec:
                self.dbufs[0][j] = term
            else:
                self.sib_out[k, j] = term
        self.sib_copy(k, dec).start()
        for j in range(self.chips):
            term = dot(operand, weights[j * 2 + self.core])
            if dec:
                self.dbufs[4][j] = term
            else:
                self.keep[par, j] = term

    def pair_sum(self, k):
        par = lax.rem(k, 2)
        self.sib_copy(k, False).wait_recv()
        for j in range(self.chips):
            self.sums[k, j] = (self.keep[par, j] + self.sib_in[k, j].astype(F32)).astype(BF)

    def sum_copy(self, k, j, right):
        place = j if right else jnp.where(self.chip - 1 == j, self.chips, j)
        return self.remote(self.sums.at[k, j], self.z_in.at[k, place], self.z_s.at[k, j], self.z_r.at[k, place],
                           self.beside(right))

    def sum_wait(self, k, place):
        ref = self.z_in.at[k, place]
        self.remote(ref, ref, self.z_s.at[k, 0], self.z_r.at[k, place], self.sibling()).wait_recv()

    def chain(self, k, right):
        for j in reversed(range(self.chips)) if right else range(self.chips):
            @pl.when(self.chip < j if right else self.chip > j)
            def _():
                @pl.when(self.has(not right))
                def _():
                    self.sum_wait(k, j)
                    self.sums[k, j] = (self.sums[k, j].astype(F32) + self.z_in[k, j].astype(F32)).astype(BF)
                self.sum_copy(k, j, right).start()

    def total(self, k, out_ref):
        self.tot[...] = self.x[self.rows(k), :].astype(F32) + self.sums[k, self.chip].astype(F32)
        for right, place in ((False, self.chip), (True, self.chips)):
            @pl.when(self.has(right))
            def _():
                self.sum_wait(k, place)
                self.tot[...] += self.z_in[k, place].astype(F32)
        out_ref[self.rows(k), :] = self.tot[...].astype(BF)

    def dz_copy(self, o):
        j, dev = self.far(o)
        return self.remote(self.dbufs[2].at[j], self.dbufs[3].at[self.chip], self.dz_s.at[o],
                           self.dz_r.at[self.chip], dev)

    def dpair_sum(self):
        b = self.dbufs
        self.sib_copy(self.count, True).wait_recv()
        for o in list(range(1, self.chips)) + [0]:
            j = self.far(o)[0]
            b[2][j] = (b[4][j] + b[1][j].astype(F32)).astype(BF)
            if o:
                self.dz_copy(o).start()

    def dtotal(self, out_ref):
        b = self.dbufs
        acc = self.d[...].astype(F32) + b[2][self.chip].astype(F32)
        for o in range(1, self.chips):
            j, dev = self.far(o)
            ref = b[3].at[j]
            self.remote(ref, ref, self.dz_s.at[o], self.dz_r.at[j], dev).wait_recv()
            acc = acc + b[3][j].astype(F32)
        out_ref[...] = acc[:out_ref.shape[0]].astype(BF)
        for o in range(self.chips):
            self.dgather_copy(o).wait_send()
        for o in range(1, self.chips):
            self.drelay_copy(o).wait_send()
            self.dz_copy(o).wait_send()
        self.sib_copy(self.count, True).wait_send()

    def finish(self, k):
        for h in range(self.chips):
            self.each_send(k, h, "wait")
        self.sib_copy(k, False).wait_send()
        for j in range(self.chips):
            for right in (True, False):
                @pl.when(self.chip < j if right else self.chip > j)
                def _():
                    self.sum_copy(k, j, right).wait_send()

    def run(self, work, out_ref, dout_ref, lead, before=None, hooks=()):
        count, chips = self.count, self.chips

        def at(k, action):
            @pl.when((k >= 0) & (k < count))
            def _():
                action(k)

        self.enter()
        if before is not None:
            before()
        self.dgather_start()

        def body(step, c):
            i = step - lead
            for h in reversed(range(chips)):
                at(i + lead - h, functools.partial(self.hop, h=h))
            for when, action in hooks:
                pl.when(i == when)(action)
            pl.when(i == 1)(self.drelay)

            def compute(k):
                self.gather_done(k)
                work(k, False)
            at(i, compute)

            @pl.when(i == 2)
            def _():
                self.dgather_done()
                work(count, True)
            pl.when(i == 3)(self.dpair_sum)
            at(i - 1, self.pair_sum)
            at(i - 1 - self.chip, functools.partial(self.chain, right=True))
            at(i - chips + self.chip, functools.partial(self.chain, right=False))
            at(i - chips - 1, functools.partial(self.total, out_ref=out_ref))
            return c

        lax.fori_loop(0, count + lead + chips + 1, body, 0)
        self.dtotal(dout_ref)
        lax.fori_loop(0, count, lambda k, c: (self.finish(k), c)[1], 0)


def gates(z):
    u = jnp.exp(-jnp.abs(z))
    big = 1.0 / (1.0 + u)
    small = u * big
    logf = jnp.minimum(z, 0.0) - jnp.log1p(u)
    return logf, jnp.where(z >= 0, small, big), jnp.where(z >= 0, big, small)


def head_norm(o, gain):
    return (o * lax.rsqrt(jnp.mean(o * o, axis=-1, keepdims=True) + EPS) * gain).astype(BF)


def mix_kernel(heads, plen, lengths, x_ref, d_ref, wf_ref, wo_ref, bias_ref, gain_ref, sums_ref, dst_ref, wgu_ref, wd_ref,
               out_ref, dout_ref, states_ref, next_ref, gu_out, down_out,
               wf, wo, gu_ref, down_ref, dpad, state, ws_s, ws_r, own_s, full, dfull, *rest):
    ex = Exchange(x_ref, dpad, full, dfull, rest[:5], rest[5:10], rest[10], rest[11:], extra_peers=True)
    spare = jnp.zeros((DEC - d_ref.shape[0], d_ref.shape[1]), F32)
    dpad[...] = jnp.concatenate([d_ref[...].astype(F32), spare], axis=0).astype(BF)
    n_mlp, feat = full.shape[0], full.shape[2]
    per = wf_ref.shape[0] // feat
    dk = dst_ref.shape[-1]
    decodes = dst_ref.shape[0]
    req = ex.req

    square = ex.n_req == 4
    if square:
        x_peer = req + 1 - 2 * (req % 2)
        y_peer = lax.rem(req + 2, 4)
        cross = lax.rem(x_peer + 2, 4)
        ways, relays = (0, 1), (2, 3)
        targets = (x_peer, y_peer, y_peer, x_peer)
    else:
        ways, relays = tuple(range(1, ex.n_req)), ()

    def place(i, owner, half=None):
        buf = (wf, wo, gu_out, down_out)[i]
        rows = slice(None)
        if half is not None:
            n = buf.shape[2 if i == 2 else 1] // 2
            rows = pl.ds(half * n, n)
        if i == 0:
            return buf.at[owner, rows]
        if i == 2:
            return buf.at[owner, :, rows]
        return buf.at[pl.ds(owner * per, per), rows]

    def w_send(i, way):
        if way in relays:
            ref = place(i, (x_peer, y_peer)[way - 2], way - 2)
            return ex.remote(ref, ref, ws_s.at[i, way], ws_r.at[i, way], (targets[way], ex.me))
        src = gu_ref if i == 2 else down_ref if i == 3 else place(i, req)
        peer = targets[way] if square else lax.rem(req + way, ex.n_req)
        at = way if square else req
        return ex.remote(src, place(i, req), ws_s.at[i, way], ws_r.at[i, at], (peer, ex.me))

    def w_wait(i, way):
        if way in relays:
            ref, at = place(i, cross, way - 2), way
        elif square:
            ref, at = place(i, targets[way]), way
        else:
            at = lax.rem(req + way, ex.n_req)
            ref = place(i, at)
        peer = lax.rem(req + 1, ex.n_req)
        ex.remote(ref, ref, ws_s.at[i, way], ws_r.at[i, at], (peer, ex.me)).wait_recv()

    def w_all(items, which, act):
        for i in items:
            for way in which:
                if act == "start":
                    w_send(i, way).start()
                elif act == "sent":
                    w_send(i, way).wait_send()
                else:
                    w_wait(i, way)

    def own_copies():
        return (pltpu.make_async_copy(gu_ref, gu_out.at[req], own_s.at[0]),
                pltpu.make_async_copy(down_ref, down_out.at[pl.ds(req * per, per)], own_s.at[1]))

    def before():
        wf[req] = wf_ref[...].astype(BF)
        for p in range(per):
            wo[req * per + p] = wo_ref[:, p * feat:(p + 1) * feat].astype(BF)
        w_all((0, 1), ways, "start")

    def fio_relay():
        w_all((0,), ways, "wait")
        w_all((0,), relays, "start")

    def out_relay():
        hidden = wd_ref.shape[0]
        gu_ref[0] = wgu_ref[:, :hidden].astype(BF)
        gu_ref[1] = wgu_ref[:, hidden:].astype(BF)
        for p in range(per):
            down_ref[p] = wd_ref[:, p * feat:(p + 1) * feat].astype(BF)
        w_all((1,), ways, "wait")
        w_all((1,), relays, "start")
        w_all((2, 3), ways, "start")
        for copy in own_copies():
            copy.start()

    def second_relay():
        w_all((2, 3), ways, "wait")
        w_all((2, 3), relays, "start")

    def mixing(block):
        acc = None
        for s in range(n_mlp):
            term = dot(block(s), wf[s // per, (s % per) * feat:(s % per + 1) * feat, :])
            acc = term if acc is None else acc + term
        return acc

    def step(m, k, sub):
        p = (k * CHUNK) // plen
        row0 = lax.rem(k * CHUNK, plen) + sub * SUB
        row = row0 + lax.broadcasted_iota(jnp.int32, (SUB, dk), 0)
        alive = row < lengths[p]
        lg, kg = [], []
        for h in range(heads):
            z = m[:, h * 3 * dk:h * 3 * dk + dk] + bias_ref[:, h * dk:(h + 1) * dk]
            logf, key, _ = gates(z)
            lg.append(jnp.where(alive, logf, 0.0))
            kg.append(jnp.where(alive, key, 0.0))
        lf = jnp.concatenate(lg, axis=1) if heads > 1 else lg[0]
        hi = lf.astype(BF)
        lo = (lf - hi.astype(F32)).astype(BF)
        decays = jnp.exp(dot(sums_ref[...], jnp.concatenate([hi, lo], axis=0)))
        t = lax.broadcasted_iota(jnp.int32, (SUB, SUB), 0)
        s = lax.broadcasted_iota(jnp.int32, (SUB, SUB), 1)
        outs = []
        for h in range(heads):
            cols = slice(h * dk, (h + 1) * dk)
            v = m[:, h * 3 * dk + dk:h * 3 * dk + 2 * dk]
            q = m[:, h * 3 * dk + 2 * dk:h * 3 * dk + 3 * dk]
            k_ = kg[h]
            v16 = v.astype(BF)
            head = decays[0:SUB, cols]
            tail = decays[SUB:2 * SUB, cols]
            old = jnp.where(row0 == 0, 0.0, state[h])
            o = dot((q * head).astype(BF), old.astype(BF), ((1,), (1,)))
            scores = None
            for level in range(LEVELS, 0, -1):
                e = decays[(level + 1) * SUB:(level + 2) * SUB, cols]
                right = (lax.broadcasted_iota(jnp.int32, (SUB, dk), 0) >> (level - 1)) & 1
                qt = jnp.where(right == 1, q * e, 0.0).astype(BF)
                kt = jnp.where(right == 1, 0.0, k_ * e).astype(BF)
                term = dot(qt, kt, ((1,), (1,)))
                if level == LEVELS:
                    scores = term
                else:
                    scores = scores + jnp.where((t >> level) == (s >> level), term, 0.0)
            o = o + dot(scores.astype(BF), v16)
            o = o + jnp.sum(q * k_, axis=-1, keepdims=True) * v
            outs.append(jnp.where(alive, o, 0.0))
            new = old * head[SUB - 1:SUB, :] + dot(v16, (k_ * tail).astype(BF), ((0,), (0,)))
            state[h] = new
            states_ref[p, h] = new.T
        return outs

    def normed(outs):
        rows = [head_norm(o, gain_ref[:, h * dk:(h + 1) * dk]) for h, o in enumerate(outs)]
        return jnp.concatenate(rows, axis=1) if heads > 1 else rows[0]

    def decode(m):
        outs = []
        pad = jnp.zeros((dk - DEC, dk), F32)
        for h in range(heads):
            z = m[:, h * 3 * dk:h * 3 * dk + dk] + bias_ref[:, h * dk:(h + 1) * dk]
            _, key, f = gates(z)
            v = m[:, h * 3 * dk + dk:h * 3 * dk + 2 * dk]
            q = m[:, h * 3 * dk + 2 * dk:h * 3 * dk + 3 * dk]
            f_t = jnp.concatenate([f, pad], axis=0).T
            k_t = jnp.concatenate([key, pad], axis=0).T
            q_t = jnp.concatenate([q, pad], axis=0).T
            rows = []
            for n in range(decodes):
                new = f_t[:, n:n + 1] * dst_ref[n, h] + k_t[:, n:n + 1] * v[n:n + 1, :]
                next_ref[n, h] = new
                rows.append(jnp.sum(q_t[:, n:n + 1] * new, axis=0, keepdims=True))
            rows.append(jnp.zeros((DEC - decodes, dk), F32))
            outs.append(jnp.concatenate(rows, axis=0))
        return normed(outs)

    def work(k, dec):
        if dec:
            m = mixing(lambda s: dfull[s])
            ex.share(k, decode(m), wo, True)
            return

        @pl.when(k == 0)
        def _():
            w_all((0,), relays, "wait")
        m = mixing(lambda s: full[s, ex.rows(k), :])
        pieces = [normed(step(m[i * SUB:(i + 1) * SUB], k, i)) for i in range(CHUNK // SUB)]

        @pl.when(k == 0)
        def _():
            w_all((1,), relays, "wait")
        ex.share(k, jnp.concatenate(pieces, axis=0), wo)

    lead = max(ex.chips, ex.count * 3 // 4)
    hooks = ((lead // 3 - lead, fio_relay), (lead // 2 - lead, out_relay), (ex.count // 2, second_relay))
    ex.run(work, out_ref, dout_ref, lead, before, hooks)
    w_all((2, 3), relays, "wait")
    for i in range(4):
        w_all((i,), ways + relays, "sent")
    for copy in own_copies():
        copy.wait()


def mlp_kernel(x_ref, d_ref, gain_ref, wgu, wd, out_ref, dout_ref, full, dfull, *rest):
    ex = Exchange(x_ref, d_ref, full, dfull, rest[:5], rest[5:10], rest[10], rest[11:])
    n_mlp, feat = full.shape[0], full.shape[2]
    per = wgu.shape[2] // feat
    width = n_mlp * feat

    def work(k, dec):
        def block(s):
            return (dfull[s] if dec else full[s, ex.rows(k), :]).astype(F32)
        total = None
        for s in range(n_mlp):
            x = block(s)
            part = jnp.sum(x * x, axis=-1, keepdims=True)
            total = part if total is None else total + part
        scale = lax.rsqrt(total / width + EPS)
        gate = up = None
        for s in range(n_mlp):
            x = (block(s) * scale * gain_ref[:, s * feat:(s + 1) * feat]).astype(BF)
            part = slice((s % per) * feat, (s % per + 1) * feat)
            g = dot(x, wgu[s // per, 0, part, :])
            u = dot(x, wgu[s // per, 1, part, :])
            gate = g if gate is None else gate + g
            up = u if up is None else up + u
        hidden = (gate / (1.0 + jnp.exp(-gate)) * up).astype(BF)
        ex.share(k, hidden, wd, dec)

    ex.run(work, out_ref, dout_ref, ex.chips)


def exchange_scratch(n_mlp, count, feat):
    chips = n_mlp // 2
    dma = pltpu.SemaphoreType.DMA
    big = pltpu.VMEM((count, chips, CHUNK, feat), BF)
    small = pltpu.VMEM((chips, DEC, feat), BF)
    return [
        pltpu.VMEM((n_mlp, count * CHUNK, feat), BF),
        pltpu.VMEM((n_mlp, DEC, feat), BF),
        big, big, big, pltpu.VMEM((count, chips + 1, CHUNK, feat), BF), pltpu.VMEM((2, chips, CHUNK, feat), F32),
        small, small, small, small, pltpu.VMEM((chips, DEC, feat), F32),
        pltpu.VMEM((CHUNK, feat), F32),
        dma((count, chips + 1)), dma((count, chips)), dma((count, n_mlp)),
        dma((chips,)), dma((chips,)), dma((n_mlp,)),
        dma((count + 1,)), dma((count + 1,)), dma((count, chips)), dma((count, chips + 1)),
        dma((chips,)), dma((chips,)),
    ]


def on_device(n_req, n_mlp, prompt_tokens, decode_tokens, prompt_lengths, decode_states, w_fio, forget_bias,
              head_gain, w_out, mlp_gain, w_gu, w_down):
    prompts, plen, feat = prompt_tokens.shape
    decodes, heads, dk, _ = decode_states.shape
    rows = prompts * plen
    count = rows // CHUNK
    per = w_fio.shape[0] // feat
    vmem = pl.BlockSpec(memory_space=pltpu.VMEM)
    anywhere = pl.BlockSpec(memory_space=pl.ANY)
    x = prompt_tokens.reshape(rows, feat)
    params = functools.partial(pltpu.CompilerParams, has_side_effects=True, vmem_limit_bytes=58 * 2**20)
    hidden = w_down.shape[0]

    gu_block = (2, w_gu.shape[0], hidden)
    down_block = (per, hidden, feat)

    dma = pltpu.SemaphoreType.DMA
    residual, dresidual, states, after, gu, down = pl.pallas_call(
        functools.partial(mix_kernel, heads, plen),
        out_shape=(
            jax.ShapeDtypeStruct((rows, feat), BF),
            jax.ShapeDtypeStruct((DEC, feat), BF),
            jax.ShapeDtypeStruct((prompts, heads, dk, dk), F32),
            jax.ShapeDtypeStruct((decodes, heads, dk, dk), F32),
            jax.ShapeDtypeStruct((n_req,) + gu_block, BF),
            jax.ShapeDtypeStruct((n_mlp,) + down_block[1:], BF),
        ),
        in_specs=[pl.BlockSpec(memory_space=pltpu.SMEM)] + [vmem] * 10,
        out_specs=(vmem,) * 4 + (anywhere,) * 2,
        scratch_shapes=[
            pltpu.VMEM((n_req,) + w_fio.shape, BF),
            pltpu.VMEM((n_mlp, heads * dk, feat), BF),
            pltpu.VMEM(gu_block, BF),
            pltpu.VMEM(down_block, BF),
            pltpu.VMEM((DEC, feat), BF),
            pltpu.VMEM((heads, dk, dk), F32),
            dma((4, n_req)), dma((4, n_req)), dma((2,)),
        ] + exchange_scratch(n_mlp, count, feat),
        compiler_params=params(collective_id=0),
        name="mix",
    )(prompt_lengths, x, decode_tokens, w_fio, w_out, forget_bias.reshape(1, -1), head_gain.reshape(1, -1),
      jnp.asarray(decay_sums(), BF), decode_states, w_gu, w_down)

    out, dout = pl.pallas_call(
        mlp_kernel,
        out_shape=(jax.ShapeDtypeStruct((rows, feat), BF), jax.ShapeDtypeStruct((decodes, feat), BF)),
        in_specs=[vmem] * 5,
        out_specs=(vmem,) * 2,
        scratch_shapes=exchange_scratch(n_mlp, count, feat),
        compiler_params=params(collective_id=1),
        name="mlp",
    )(residual, dresidual, mlp_gain.reshape(1, -1), gu, down)
    return out.reshape(prompts, plen, feat), dout, states, after


def solution(mesh):
    placed = (
        P("req", None, "mlp"),
        P("req", "mlp"),
        P("req"),
        P("req", "mlp", None, None),
        P("req", "mlp"),
        P("mlp"),
        P("mlp"),
        P("mlp", "req"),
        P(),
        P("req", "mlp"),
        P("mlp", "req"),
    )
    return jax.shard_map(
        functools.partial(on_device, mesh.shape["req"], mesh.shape["mlp"]),
        mesh=mesh,
        in_specs=placed,
        out_specs=(
            P("req", None, "mlp"),
            P("req", "mlp"),
            P("req", "mlp", None, None),
            P("req", "mlp", None, None),
        ),
        check_vma=False,
    )
```
